256 devices in a mesh: step: 32 (over y, z), head: 8 (over x, core).
Axes of the slice: x: 4, y: 4, z: 8, core: 2. Of those that a mesh axis runs over, the one named last changes fastest.
Arguments:
- guesses: float32 [32, 256, 64], P('step', 'head'), may hold values from -6 to 6
- step_ids: int32 [32], P('step'), may hold values from 0 to 63
- step_sizes: float32 [32], P('step'), may hold values from 0.02 to 0.1
- slide: int32 [1], replicated, may hold values from 1 to 31
- offsets: int32 [256, 2], replicated, may hold values from 0 to 7
- mod_table: float32 [64, 3, 3072], replicated, may hold values from -3 to 3
- w_in: bfloat16 [64, 3072], replicated, may hold values from -0.75 to 0.75
- w_qkv: bfloat16 [3072, 9216], P(None, 'head')
- qk_gain: float32 [2, 128], replicated, may hold values from 0.6 to 4.5
- w_out: bfloat16 [3072, 3072], P('head'), may hold values from -0.109375 to 0.109375
- w_fin: bfloat16 [3072, 64], replicated, may hold values from -0.109375 to 0.109375
Outputs:
- slid: float32 [32, 256, 64], P('step', 'head')
The draws below stay inside these ranges and needn't reach their ends.
All inputs are finite; a program needn't handle non-finite values.
Results may differ from the reference program's by a relative error of at most 0.0033.
Values may be sent and summed in bfloat16 or wider, within the bound.
No kernel may reach another device: no remote copies, remote signals or barrier semaphores. Data moves between devices by JAX's collectives and lax.ppermute only.
A program may use at most 64 MiB of HBM per device.

```python
import math
import jax
import jax.numpy as jnp
from jax import lax

D = 3072
HEADS = 24
HD = 128
C = 64
S = 256
GRID_W = 16
ROT_DIM = 56
T_TABLE = 64
SWEEPS = 2
W = 32
HL = 3
N_STEP = 32
N_HEAD = 8


def draw_w_qkv(key, part):
    key = jax.random.fold_in(key, 11)
    query = jax.random.normal(jax.random.fold_in(key, 1), (D, HEADS, 1, HD), jnp.float32)
    keys = jax.random.normal(jax.random.fold_in(key, 2), (D, HEADS, 1, HD), jnp.float32)
    values = jax.random.normal(jax.random.fold_in(key, 3), (D, HEADS, 1, HD), jnp.float32)
    whole = jnp.concatenate([query, keys, values], axis=2) * D ** (-0.5)
    return whole.reshape(D, HEADS * 3 * HD).astype(jnp.bfloat16)


def draw_qk_gain(key, part):
    key = jax.random.fold_in(key, 12)
    return jax.random.uniform(key, (2, HD), jnp.float32, 0.6, 1.6)


def with_ends(entries, rng, low, top_value):
    place = [jax.random.randint(jax.random.fold_in(rng, axis), (), 0, length) for axis, length in enumerate(entries.shape)]
    longest = entries.shape.index(max(entries.shape))
    neighbour = place[:longest] + [(place[longest] + 1) % entries.shape[longest]] + place[longest + 1:]
    return entries.at[tuple(place)].set(low).at[tuple(neighbour)].set(top_value)


def block_levels(stream_key, extent, split, low, top_value):
    level = 1.0
    for position, shards_of in split:
        draws = jax.random.uniform(jax.random.fold_in(jax.random.fold_in(stream_key, 6), position), (shards_of,), jnp.float32, low / len(split), top_value / len(split))
        level = level * jnp.repeat(jnp.exp(draws), extent[position] // shards_of).reshape((-1,) + (1,) * (len(extent) - 1 - position))
    return level


def normal_values(rng, extent, deviation, most, split=(), kind=jnp.bfloat16):
    entries = deviation * jax.random.normal(rng, extent, jnp.float32)
    if split:
        entries = entries * block_levels(rng, extent, split, -0.22, 0.18)
    return jnp.clip(entries, -most, most).astype(kind)


def setup_inputs(seed: int = 0) -> dict:
    splits = jax.random.split(jax.random.key(seed), 12)
    return {
        "guesses": normal_values(splits[0], (W, S, C), 1.0, 6.0, ((0, 32), (1, 8)), jnp.float32),
        "step_ids": with_ends(jax.random.randint(splits[1], (W,), 0, T_TABLE), jax.random.fold_in(splits[1], 1), 0, T_TABLE - 1).astype(jnp.int32),
        "step_sizes": jnp.clip(jnp.exp(math.log(0.1) - 1.609438 * jax.random.uniform(splits[2], (W,), jnp.float32) ** block_levels(splits[2], (W,), ((0, 32),), -0.2, 0.2)), 0.02, 0.1),
        "slide": jax.random.randint(splits[3], (1,), 1, N_STEP).astype(jnp.int32),
        "offsets": with_ends(jax.random.randint(splits[4], (S, 2), 0, 8), jax.random.fold_in(splits[4], 1), 0, 7).astype(jnp.int32),
        "mod_table": normal_values(splits[5], (T_TABLE, 3, D), 0.5, 3.0, (), jnp.float32),
        "w_in": normal_values(splits[6], (C, D), C ** -0.5, 0.75),
        "w_qkv": draw_w_qkv(jax.random.fold_in(splits[11], 71), 0),
        "qk_gain": draw_qk_gain(jax.random.fold_in(splits[11], 71), 0),
        "w_out": normal_values(splits[9], (HEADS * HD, D), (HEADS * HD) ** -0.5, 0.109375, ((0, 8),)),
        "w_fin": normal_values(splits[10], (D, C), D ** -0.5, 0.109375),
    }


def layer_norm(x):
    mean = lax.optimization_barrier(jnp.mean(x, axis=-1, keepdims=True))
    centered = x - mean
    var = lax.optimization_barrier(jnp.mean(centered * centered, axis=-1, keepdims=True))
    return centered * lax.rsqrt(var + 1e-06)

def rotary_angles(offsets, count, head_dim):
    index = jnp.arange(count, dtype=jnp.int32)
    rows = (index // GRID_W + offsets[:, 0]).astype(jnp.float32)
    cols = (index % GRID_W + offsets[:, 1]).astype(jnp.float32)
    freq = 10000.0 ** (-jnp.arange(ROT_DIM // 2, dtype=jnp.float32) * 2.0 / ROT_DIM)
    still = jnp.zeros((count, (head_dim - 2 * ROT_DIM) // 2), jnp.float32)
    return jnp.concatenate([still, rows[:, None] * freq, cols[:, None] * freq], axis=1)

def rotate(x, angles):
    count, heads, head_dim = x.shape
    pairs = x.reshape(count, heads, head_dim // 2, 2)
    cosine = jnp.cos(angles)[:, None, :]
    sine = jnp.sin(angles)[:, None, :]
    first = pairs[..., 0]
    second = pairs[..., 1]
    out = jnp.stack([first * cosine - second * sine, first * sine + second * cosine], axis=-1)
    return out.reshape(count, heads, head_dim)

def rms_gain(x, gain):
    return x * lax.rsqrt(lax.optimization_barrier(jnp.mean(x * x, axis=-1, keepdims=True)) + 1e-06) * gain

def drift_of(state, step_id, step_size, angles, mod_table, w_in, w_qkv, qk_gain, w_out, w_fin):
    mod = mod_table[step_id]
    embed = jnp.dot(state.astype(jnp.bfloat16), w_in, preferred_element_type=jnp.float32)
    features = (layer_norm(embed) * (1.0 + mod[1]) + mod[0]).astype(jnp.bfloat16)
    qkv = jnp.dot(features, w_qkv, preferred_element_type=jnp.float32).reshape(S, HEADS, 3, HD)
    query = rotate(rms_gain(qkv[:, :, 0], qk_gain[0]), angles).astype(jnp.bfloat16)
    keys = rotate(rms_gain(qkv[:, :, 1], qk_gain[1]), angles).astype(jnp.bfloat16)
    values = qkv[:, :, 2].astype(jnp.bfloat16)
    scores = jnp.einsum('shd,thd->hst', query.astype(jnp.float32), keys.astype(jnp.float32)) / math.sqrt(HD)
    probs = jax.nn.softmax(scores, axis=-1).astype(jnp.bfloat16)
    heads_out = jnp.einsum('hst,thd->shd', probs.astype(jnp.float32), values.astype(jnp.float32))
    heads_out = heads_out.astype(jnp.bfloat16).reshape(S, N_HEAD, HL * HD)
    grouped = w_out.reshape(N_HEAD, HL * HD, D)
    partial_value = jnp.einsum('sgk,gkd->gsd', heads_out.astype(jnp.float32), grouped.astype(jnp.float32)).astype(jnp.bfloat16)
    attn = lax.optimization_barrier(jnp.sum(partial_value.astype(jnp.float32), axis=0))
    hres = embed + mod[2] * attn
    normed = layer_norm(hres).astype(jnp.bfloat16)
    return step_size * jnp.dot(normed, w_fin, preferred_element_type=jnp.float32)

def reference(guesses, step_ids, step_sizes, slide, offsets, mod_table, w_in, w_qkv, qk_gain, w_out, w_fin):
    angles = rotary_angles(offsets, S, HD)
    states = guesses
    for sweep in range(SWEEPS):
        drifts = lax.map(lambda item: drift_of(item[0], item[1], item[2], angles, mod_table, w_in, w_qkv, qk_gain, w_out, w_fin), (states, step_ids, step_sizes))
        before = jnp.concatenate([jnp.zeros((1, S, C), jnp.float32), jnp.cumsum(drifts, axis=0)[:-1]], axis=0)
        states = states[0][None] + before
    target = jnp.minimum(jnp.arange(W, dtype=jnp.int32) + slide[0], W - 1)
    return states[target]
```

```python
import math

import jax
import jax.numpy as jnp
import numpy as np
from jax import lax
from jax.experimental import pallas as pl
from jax.experimental.pallas import tpu as pltpu
from jax.sharding import Mesh
from jax.sharding import PartitionSpec as P

NY, NZ, NX, NC = 4, 8, 4, 2
D = 3072
HD = 128
HL = 3
C = 64
S = 256
ROWS = 32
GRID_W = 16
ROT_DIM = 56
EPS = 1e-06
BF = jnp.bfloat16
F32 = jnp.float32
MIB = 1024 * 1024

VM = pl.BlockSpec(memory_space=pltpu.VMEM)
SM = pl.BlockSpec(memory_space=pltpu.SMEM)
ANY = pl.BlockSpec(memory_space=pl.ANY)


def pack(x):
    return jnp.concatenate([x[:16], x[16:]], axis=1)


def unpack(x):
    return jnp.concatenate([x[:, :C], x[:, C:]], axis=0)


def tables(offsets, qk_gain):
    index = jnp.arange(S, dtype=jnp.int32)
    rows = (index // GRID_W + offsets[:, 0]).astype(F32)
    cols = (index % GRID_W + offsets[:, 1]).astype(F32)
    freq = 10000.0 ** (-jnp.arange(ROT_DIM // 2, dtype=F32) * 2.0 / ROT_DIM)
    still = jnp.zeros((S, (HD - 2 * ROT_DIM) // 2), F32)
    angles = jnp.concatenate([still, rows[:, None] * freq, cols[:, None] * freq], axis=1)
    angles = jnp.repeat(angles, 2, axis=1)
    sign = jnp.where(jnp.arange(HD) % 2 == 0, -1.0, 1.0).astype(F32)
    cosine = jnp.cos(angles)
    sine = jnp.sin(angles) * sign
    swapped = qk_gain.reshape(2, HD // 2, 2)[:, :, ::-1].reshape(2, HD)
    whole = jnp.stack(
        [cosine * qk_gain[0], sine * swapped[0], cosine * qk_gain[1], sine * swapped[1]]
    )
    return whole.reshape(4, 8, ROWS, HD)


def block_body(place, chunk_of, tab, w_in, mod, w_qkv, h_out, zs, es, fs, wv, qs, sems):
    my_x, my_c = place[2], place[3]
    copies = []
    for head in range(HL):
        cut = pl.ds(head * 3 * HD, 3 * HD)
        copy = pltpu.make_async_copy(w_qkv.at[:, cut], wv.at[:, cut], sems.at[head])
        copy.start()
        copies.append(copy)
    order = []
    for r in range(8):
        where = ((my_x + r % 4) % 4) * 2 + (my_c + r // 4) % 2
        order.append(where)
        piece = chunk_of(where)
        zs[32 * r : 32 * r + 16, :] = piece[:, :C]
        zs[32 * r + 16 : 32 * r + 32, :] = piece[:, C:]
    z = zs[...]
    for j in range(6):
        cut = slice(j * 512, j * 512 + 512)
        es[:, cut] = jnp.dot(z, w_in[:, cut], preferred_element_type=F32)

    def norm_rows(i, carry):
        at = pl.ds(pl.multiple_of(i * ROWS, ROWS), ROWS)
        e = es[at, :]
        mean = jnp.sum(e, axis=-1, keepdims=True) * (1.0 / D)
        e = e - mean
        var = jnp.sum(e * e, axis=-1, keepdims=True) * (1.0 / D)
        f = e * lax.rsqrt(var + EPS) * (1.0 + mod[1:2, :]) + mod[0:1, :]
        fs[at, :] = f.astype(BF)
        return carry

    lax.fori_loop(0, 8, norm_rows, 0)
    lane = lax.broadcasted_iota(jnp.int32, (ROWS, HD), 1)
    even = lane % 2 == 0

    def turned(x, tc, ts):
        r = lax.rsqrt(jnp.mean(x * x, axis=-1, keepdims=True) + EPS)
        swap = jnp.where(even, pltpu.roll(x, HD - 1, 1), pltpu.roll(x, 1, 1))
        return ((x * tc + swap * ts) * r).astype(BF)

    for head in range(HL):
        copies[head].wait()
        base = head * 3 * HD
        qkv = jnp.dot(fs[...], wv[:, base : base + 3 * HD], preferred_element_type=F32)
        for r in range(8):
            rows = slice(32 * r, 32 * r + 32)
            where = order[r]
            qs[0, rows, :] = turned(qkv[rows, :HD], tab[0, where], tab[1, where])
            qs[1, rows, :] = turned(qkv[rows, HD : 2 * HD], tab[2, where], tab[3, where])
            qs[2, rows, :] = qkv[rows, 2 * HD :].astype(BF)
        scores = lax.dot_general(
            qs[0], qs[1], (((1,), (1,)), ((), ())), preferred_element_type=F32
        )
        top = jnp.max(scores, axis=-1, keepdims=True)
        p = jnp.exp((scores - top) * (1.0 / math.sqrt(HD)))
        p = p / jnp.sum(p, axis=-1, keepdims=True)
        out = jnp.dot(p.astype(BF), qs[2], preferred_element_type=F32)
        h_out[:, head * HD : head * HD + HD] = out.astype(BF)


def first_kernel(place, zg, tab, w_in, mod, w_qkv, h_out, *scratch):
    block_body(place, lambda i: zg[i], tab, w_in, mod, w_qkv, h_out, *scratch)


def second_kernel(place, zg, parts, tab, w_in, mod, w_qkv, h_out, z_out, *scratch):
    start = place[0] * NZ + place[1] == 0

    def chunk_of(i):
        x, c = i // 2, i % 2
        total = parts[0, x, c] + parts[1, x, c] + parts[2, x, c] + parts[3, x, c]
        return jnp.where(start, zg[i].astype(F32), total).astype(BF)

    z_out[...] = chunk_of(place[2] * 2 + place[3])
    block_body(place, chunk_of, tab, w_in, mod, w_qkv, h_out, *scratch)


BLOCK_SCRATCH = [
    pltpu.VMEM((S, C), BF),
    pltpu.VMEM((S, D), F32),
    pltpu.VMEM((S, D), BF),
    pltpu.VMEM((D, HL * 3 * HD), BF),
    pltpu.VMEM((3, S, HD), BF),
    pltpu.SemaphoreType.DMA((HL,)),
]
BLOCK_PARAMS = pltpu.CompilerParams(vmem_limit_bytes=32 * MIB)


def out_kernel(mine, peer, w_mine, w_peer, first, *others):
    for j in range(6):
        cut = slice(j * 512, j * 512 + 512)
        part = jnp.dot(mine[...], w_mine[:, cut], preferred_element_type=F32)
        part += jnp.dot(peer[...], w_peer[:, cut], preferred_element_type=F32)
        part = part.astype(BF)
        first[:, cut] = part[:ROWS]
        for k in range(3):
            others[k][:, cut] = part[ROWS * (k + 1) : ROWS * (k + 2)]


def drift_kernel(place, size, z, zstart, p0, p1, p2, p3, w_in, mod, w_fin, out):
    e = jnp.dot(unpack(z[...]), w_in[...], preferred_element_type=F32)
    attn = p0[...].astype(F32) + p1[...].astype(F32) + p2[...].astype(F32) + p3[...].astype(F32)
    h = e + mod[2:3, :] * attn
    mean = jnp.sum(h, axis=-1, keepdims=True) * (1.0 / D)
    h = h - mean
    var = jnp.sum(h * h, axis=-1, keepdims=True) * (1.0 / D)
    normed = (h * lax.rsqrt(var + EPS)).astype(BF)
    drift = size[0] * jnp.dot(normed, w_fin[...], preferred_element_type=F32)
    start = place[0] * NZ + place[1] == 0
    drift = drift + jnp.where(start, zstart[...], jnp.zeros((ROWS, C), F32))
    packed = pack(drift)
    for k in range(out.shape[0]):
        out[k] = packed


def relay_kernel(place, got, out):
    y, z = place[0], place[1]
    for to in range(NY):
        total = jnp.zeros((NC, 16, 128), F32)
        for s in range(NZ):
            keep = y * NZ + s < to * NZ + z
            total = total + jnp.where(keep, got[s], jnp.zeros((NC, 16, 128), F32))
        for x in range(NX):
            out[to, x] = total


def final_kernel(place, slide, got, out):
    target = jnp.minimum(place[0] * NZ + place[1] + slide[0], NY * NZ - 1)
    total = got[0]
    for s in range(1, NY * NZ - 1):
        total = total + jnp.where(s < target, got[s], jnp.zeros((16, 128), F32))
    out[0] = unpack(total)


def call(body, out_shape, in_specs, scratch=(), params=None):
    several = isinstance(out_shape, (list, tuple))
    return pl.pallas_call(
        body,
        out_shape=out_shape,
        in_specs=in_specs,
        out_specs=[VM] * len(out_shape) if several else VM,
        scratch_shapes=list(scratch),
        compiler_params=params or pltpu.CompilerParams(vmem_limit_bytes=24 * MIB),
    )


def shape(dims, dtype):
    return jax.ShapeDtypeStruct(dims, dtype)


def swap_cores(x):
    return lax.ppermute(x, "c", [(0, 1), (1, 0)])


def local(
    guesses, step_ids, step_sizes, slide, offsets, mod_table, w_in, w_qkv, qk_gain, w_out, w_fin
):
    place = jnp.stack([lax.axis_index(a) for a in ("y", "z", "x", "c")]).astype(jnp.int32)
    state = guesses[0]
    w_peer = swap_cores(w_out)
    z = pack(state.astype(BF))
    zg = lax.all_to_all(
        jnp.broadcast_to(z[None], (8, 16, 128)), ("x", "c"), 0, 0, tiled=True
    )
    tab = tables(offsets, qk_gain)
    mod = lax.dynamic_index_in_dim(mod_table, step_ids[0], 0, keepdims=False)

    def to_drift(h, z, copies):
        peer = swap_cores(h[S // 2 :])
        parts = call(
            out_kernel, [shape((ROWS, D), BF)] * 4, [VM] * 4
        )(h[: S // 2], peer, w_out, w_peer)
        got = [parts[0]]
        for k in (2, 1, 3):
            got.append(lax.ppermute(parts[k], "x", [(i, (i + k) % NX) for i in range(NX)]))
        return call(
            drift_kernel, shape((copies, 16, 128), F32), [SM, SM] + [VM] * 9
        )(place, step_sizes, z, state, *got, w_in, mod, w_fin)

    h = call(
        first_kernel,
        shape((S, HL * HD), BF),
        [SM, VM, VM, VM, VM, ANY],
        BLOCK_SCRATCH,
        BLOCK_PARAMS,
    )(place, zg, tab, w_in, mod, w_qkv)
    drift = to_drift(h, z, NZ * NC)
    got = lax.all_to_all(drift, ("z", "c"), 0, 0, tiled=True)
    parts = call(relay_kernel, shape((NY, NX, NC, 16, 128), F32), [SM, VM])(
        place, got.reshape(NZ, NC, 16, 128)
    )
    parts = lax.all_to_all(
        parts.reshape(NY * NX, NC, 16, 128), ("y", "x"), 0, 0, tiled=True
    ).reshape(NY, NX, NC, 16, 128)
    h, z = call(
        second_kernel,
        [shape((S, HL * HD), BF), shape((16, 128), BF)],
        [SM, VM, VM, VM, VM, VM, ANY],
        BLOCK_SCRATCH,
        BLOCK_PARAMS,
    )(place, zg, parts, tab, w_in, mod, w_qkv)
    drift = to_drift(h, z, NY * NZ)
    got = lax.all_to_all(drift, ("y", "z"), 0, 0, tiled=True)
    return call(final_kernel, shape((1, ROWS, C), F32), [SM, SM, VM])(place, slide, got)


def solution(mesh):
    grid = Mesh(mesh.devices.reshape(NY, NZ, NX, NC), ("y", "z", "x", "c"))
    step, head = ("y", "z"), ("x", "c")
    in_specs = (
        P(step, head, None),
        P(step),
        P(step),
        P(),
        P(),
        P(),
        P(),
        P(None, head),
        P(),
        P(head, None),
        P(),
    )
    out_specs = P(step, head, None)
    return jax.shard_map(local, mesh=grid, in_specs=in_specs, out_specs=out_specs, check_vma=False)
```

```python
import math

import jax
import jax.numpy as jnp
import numpy as np
from jax import lax
from jax.experimental import pallas as pl
from jax.experimental.pallas import tpu as pltpu
from jax.sharding import Mesh
from jax.sharding import PartitionSpec as P

NY, NZ, NX, NC = 4, 8, 4, 2
D = 3072
HD = 128
HL = 3
C = 64
S = 256
ROWS = 32
GRID_W = 16
ROT_DIM = 56
EPS = 1e-06
BF = jnp.bfloat16
F32 = jnp.float32
MIB = 1024 * 1024

VM = pl.BlockSpec(memory_space=pltpu.VMEM)
SM = pl.BlockSpec(memory_space=pltpu.SMEM)
ANY = pl.BlockSpec(memory_space=pl.ANY)


def pack(x):
    return jnp.concatenate([x[:16], x[16:]], axis=1)


def unpack(x):
    return jnp.concatenate([x[:, :C], x[:, C:]], axis=0)


FREQ = 10000.0 ** (-np.arange(ROT_DIM // 2) * 2.0 / ROT_DIM)
LANE_FREQ = np.zeros((2, HD), np.float32)
LANE_FREQ[0, HD - 4 * (ROT_DIM // 2) : HD - 2 * (ROT_DIM // 2)] = np.repeat(FREQ, 2)
LANE_FREQ[1, HD - 2 * (ROT_DIM // 2) :] = np.repeat(FREQ, 2)
QKV = 3 * HD
CUTS = ((0, 512), (512, 1024), (1024, 1152))


def swap_lanes(x):
    lane = lax.broadcasted_iota(jnp.int32, x.shape, len(x.shape) - 1)
    axis = len(x.shape) - 1
    return jnp.where(lane % 2 == 0, pltpu.roll(x, HD - 1, axis), pltpu.roll(x, 1, axis))


def halves(x):
    high = x.astype(BF)
    return high, (x - high.astype(F32)).astype(BF)


def prepare_kernel(offsets, freq, gain, w_in, mod, tab, wc, rows):
    index = lax.broadcasted_iota(jnp.int32, (S, 1), 0)
    row = (index // GRID_W + offsets[:, 0:1]).astype(F32)
    col = (index % GRID_W + offsets[:, 1:2]).astype(F32)
    angle = row * freq[0:1, :] + col * freq[1:2, :]
    sign = jnp.where(lax.broadcasted_iota(jnp.int32, (1, HD), 1) % 2 == 0, -1.0, 1.0)
    cosine = jnp.cos(angle)
    sine = jnp.sin(angle) * sign
    for k in range(2):
        g = gain[k : k + 1, :]
        turned = swap_lanes(jnp.broadcast_to(g, (8, HD)))[0:1]
        tab[2 * k] = (cosine * g).reshape(8, ROWS, HD)
        tab[2 * k + 1] = (sine * turned).reshape(8, ROWS, HD)
    w = w_in[...].astype(F32)
    w = w - jnp.sum(w, axis=-1, keepdims=True) * (1.0 / D)
    high, low = halves(w)
    wc[:C, :] = high
    wc[C:, :] = low
    rows[0:1, :] = 1.0 + mod[1:2, :]
    rows[1:2, :] = mod[0:1, :]
    rows[2:3, :] = mod[2:3, :]
    rows[3:, :] = jnp.zeros((5, D), F32)


def block_body(
    chunk_of, tab, wc, rows, w_qkv, mine, send, zs, es, fs, wv, qkv, qs, tabv, wcv, rowv, sems
):
    my_x, my_c = lax.axis_index("x"), lax.axis_index("c")
    order = [((my_x + r % 4) % 4) * 2 + (my_c + r // 4) % 2 for r in range(8)]
    wc_copy = pltpu.make_async_copy(wc, wcv, sems.at[3])
    wc_copy.start()
    row_copy = pltpu.make_async_copy(rows, rowv, sems.at[4])
    row_copy.start()
    copies = []
    for i, (low, high) in enumerate(CUTS):
        copy = pltpu.make_async_copy(
            w_qkv.at[:, pl.ds(low, high - low)], wv.at[:, pl.ds(low, high - low)], sems.at[i]
        )
        copy.start()
        copies.append(copy)
        if i == 0:
            tab_copies = [
                pltpu.make_async_copy(
                    tab.at[:, order[r]], tabv.at[:, pl.ds(32 * r, 32)], sems.at[5 + r]
                )
                for r in range(8)
            ]
            for copy in tab_copies:
                copy.start()
    for r in range(8):
        piece = chunk_of(order[r])
        zs[32 * r : 32 * r + 16, :] = piece[:, :C]
        zs[32 * r + 16 : 32 * r + 32, :] = piece[:, C:]
    z = zs[...]
    twice = jnp.concatenate([z, z], axis=1)
    total = jnp.zeros((S, 128), F32)
    wc_copy.wait()
    for j in range(6):
        cut = slice(j * 512, j * 512 + 512)
        e = jnp.dot(twice, wcv[:, cut], preferred_element_type=F32)
        es[:, cut] = e
        e = e * e
        total += (e[:, :128] + e[:, 128:256]) + (e[:, 256:384] + e[:, 384:])
    scale = lax.rsqrt(jnp.sum(total, axis=-1, keepdims=True) * (1.0 / D) + EPS)
    row_copy.wait()
    for j in range(6):
        cut = slice(j * 512, j * 512 + 512)
        fs[:, cut] = (es[:, cut] * scale * rowv[0:1, cut] + rowv[1:2, cut]).astype(BF)
    for copy in tab_copies:
        copy.wait()
    mean = jnp.full((2 * HD, HD), 1.0 / HD, BF)

    def turned(x, k):
        high, low = halves(x * x)
        square = jnp.dot(jnp.concatenate([high, low], axis=1), mean, preferred_element_type=F32)
        x = x * tabv[2 * k] + swap_lanes(x) * tabv[2 * k + 1]
        return (x * lax.rsqrt(square + EPS)).astype(BF)

    def attend(head):
        base = head * QKV
        for k in range(2):
            qs[head, k] = turned(qkv[:, base + k * HD : base + k * HD + HD], k)
        qs[head, 2] = qkv[:, base + 2 * HD : base + QKV].astype(BF)
        scores = lax.dot_general(
            qs[head, 0], qs[head, 1], (((1,), (1,)), ((), ())), preferred_element_type=F32
        )
        top = jnp.max(scores, axis=-1, keepdims=True)
        p = jnp.exp((scores - top) * (1.0 / math.sqrt(HD)))
        p = p * (1.0 / jnp.sum(p, axis=-1, keepdims=True))
        out = jnp.dot(p.astype(BF), qs[head, 2], preferred_element_type=F32).astype(BF)
        mine[:, head * HD : head * HD + HD] = out[: S // 2]
        send[:, head * HD : head * HD + HD] = out[S // 2 :]

    for i, (low, high) in enumerate(CUTS):
        copies[i].wait()
        qkv[:, low:high] = jnp.dot(fs[...], wv[:, low:high], preferred_element_type=F32)
        if i > 0:
            attend(i - 1)
    attend(2)


def first_kernel(zg, *rest):
    block_body(lambda i: zg[i], *rest)


def second_kernel(zg, parts, tab, wc, rows, w_qkv, mine, send, z_out, *scratch):
    start = lax.axis_index("y") * NZ + lax.axis_index("z") == 0

    def chunk_of(i):
        x, c = i // 2, i % 2
        total = parts[0, x, c] + parts[1, x, c] + parts[2, x, c] + parts[3, x, c]
        return jnp.where(start, zg[i].astype(F32), total).astype(BF)

    z_out[...] = chunk_of(lax.axis_index("x") * 2 + lax.axis_index("c"))
    block_body(chunk_of, tab, wc, rows, w_qkv, mine, send, *scratch)


BLOCK_SCRATCH = [
    pltpu.VMEM((S, C), BF),
    pltpu.VMEM((S, D), F32),
    pltpu.VMEM((S, D), BF),
    pltpu.VMEM((D, HL * QKV), BF),
    pltpu.VMEM((S, HL * QKV), F32),
    pltpu.VMEM((HL, 3, S, HD), BF),
    pltpu.VMEM((4, S, HD), F32),
    pltpu.VMEM((2 * C, D), BF),
    pltpu.VMEM((8, D), F32),
    pltpu.SemaphoreType.DMA((13,)),
]
LIMIT = 56 * MIB
PIECES = 6


def out_kernel(mine, peer, w_mine, w_peer, first, *rest):
    others, (wa, wb, sems) = rest[:3], rest[3:]
    wide = D // PIECES
    copies = []
    for j in range(PIECES):
        cut = pl.ds(j * wide, wide)
        pair = [
            pltpu.make_async_copy(w_mine.at[:, cut], wa.at[:, cut], sems.at[0, j]),
            pltpu.make_async_copy(w_peer.at[:, cut], wb.at[:, cut], sems.at[1, j]),
        ]
        for copy in pair:
            copy.start()
        copies.append(pair)
    for j in range(PIECES):
        cut = slice(j * wide, j * wide + wide)
        for copy in copies[j]:
            copy.wait()
        part = jnp.dot(mine[...], wa[:, cut], preferred_element_type=F32)
        part += jnp.dot(peer[...], wb[:, cut], preferred_element_type=F32)
        part = part.astype(BF)
        first[:, cut] = part[:ROWS]
        for k in range(3):
            others[k][:, cut] = part[ROWS * (k + 1) : ROWS * (k + 2)]


OUT_SCRATCH = [
    pltpu.VMEM((HL * HD, D), BF),
    pltpu.VMEM((HL * HD, D), BF),
    pltpu.SemaphoreType.DMA((2, PIECES)),
]


def drift_kernel(size, z, zstart, p0, p1, p2, p3, w_in, gate, w_fin, out):
    e = jnp.dot(unpack(z[...]), w_in[...], preferred_element_type=F32)
    attn = p0[...].astype(F32) + p1[...].astype(F32) + p2[...].astype(F32) + p3[...].astype(F32)
    h = e + gate[2:3, :] * attn
    mean = jnp.sum(h, axis=-1, keepdims=True) * (1.0 / D)
    h = h - mean
    var = jnp.sum(h * h, axis=-1, keepdims=True) * (1.0 / D)
    normed = (h * lax.rsqrt(var + EPS)).astype(BF)
    drift = size[0] * lax.dot_general(
        normed, w_fin[...], (((1,), (1,)), ((), ())), preferred_element_type=F32
    )
    start = lax.axis_index("y") * NZ + lax.axis_index("z") == 0
    drift = drift + jnp.where(start, zstart[...], jnp.zeros((ROWS, C), F32))
    packed = pack(drift)
    for k in range(out.shape[0]):
        out[k] = packed


def relay_kernel(got, out):
    y, z = lax.axis_index("y"), lax.axis_index("z")
    for to in range(NY):
        total = jnp.zeros((NC, 16, 128), F32)
        for s in range(NZ):
            keep = y * NZ + s < to * NZ + z
            total = total + jnp.where(keep, got[s], jnp.zeros((NC, 16, 128), F32))
        for x in range(NX):
            out[to, x] = total


def final_kernel(slide, got, out):
    here = lax.axis_index("y") * NZ + lax.axis_index("z")
    target = jnp.minimum(here + slide[0], NY * NZ - 1)
    total = got[0]
    for s in range(1, NY * NZ - 1):
        total = total + jnp.where(s < target, got[s], jnp.zeros((16, 128), F32))
    out[0] = unpack(total)


def call(body, out_shape, in_specs, scratch=()):
    several = isinstance(out_shape, (list, tuple))
    return pl.pallas_call(
        body,
        out_shape=out_shape,
        in_specs=in_specs,
        out_specs=[VM] * len(out_shape) if several else VM,
        scratch_shapes=list(scratch),
        compiler_params=pltpu.CompilerParams(vmem_limit_bytes=LIMIT),
    )


def shape(dims, dtype):
    return jax.ShapeDtypeStruct(dims, dtype)


def swap_cores(x):
    return lax.ppermute(x, "c", [(0, 1), (1, 0)])


def local(
    guesses, step_ids, step_sizes, slide, offsets, mod_table, w_in, w_qkv, qk_gain, w_out, w_fin
):
    state = guesses[0]
    w_peer = swap_cores(w_out)
    z = pack(state.astype(BF))
    zg = lax.all_to_all(jnp.broadcast_to(z[None], (8, 16, 128)), ("x", "c"), 0, 0, tiled=True)
    mod = lax.dynamic_index_in_dim(mod_table, step_ids[0], 0, keepdims=False)
    w_fin_rows = w_fin.T
    tab, wc, rows = call(
        prepare_kernel,
        [shape((4, 8, ROWS, HD), F32), shape((2 * C, D), BF), shape((8, D), F32)],
        [VM] * 5,
    )(offsets, jnp.asarray(LANE_FREQ), qk_gain, w_in, mod)
    half = shape((S // 2, HL * HD), BF)

    def to_drift(mine, send, z, copies):
        peer = swap_cores(send)
        parts = call(out_kernel, [shape((ROWS, D), BF)] * 4, [VM, VM, ANY, ANY], OUT_SCRATCH)(
            mine, peer, w_out, w_peer
        )
        got = [parts[0]]
        for k in (2, 1, 3):
            got.append(lax.ppermute(parts[k], "x", [(i, (i + k) % NX) for i in range(NX)]))
        return call(drift_kernel, shape((copies, 16, 128), F32), [SM] + [VM] * 9)(
            step_sizes, z, state, *got, w_in, rows, w_fin_rows
        )

    mine, send = call(first_kernel, [half, half], [VM] + [ANY] * 4, BLOCK_SCRATCH)(
        zg, tab, wc, rows, w_qkv
    )
    drift = to_drift(mine, send, z, NZ * NC)
    got = lax.all_to_all(drift, ("z", "c"), 0, 0, tiled=True)
    parts = call(relay_kernel, shape((NY, NX, NC, 16, 128), F32), [VM])(
        got.reshape(NZ, NC, 16, 128)
    )
    parts = lax.all_to_all(
        parts.reshape(NY * NX, NC, 16, 128), ("y", "x"), 0, 0, tiled=True
    ).reshape(NY, NX, NC, 16, 128)
    mine, send, z = call(
        second_kernel, [half, half, shape((16, 128), BF)], [VM] * 2 + [ANY] * 4, BLOCK_SCRATCH
    )(zg, parts, tab, wc, rows, w_qkv)
    drift = to_drift(mine, send, z, NY * NZ)
    got = lax.all_to_all(drift, ("y", "z"), 0, 0, tiled=True)
    return call(final_kernel, shape((1, ROWS, C), F32), [SM, VM])(slide, got)


def solution(mesh):
    grid = Mesh(mesh.devices.reshape(NY, NZ, NX, NC), ("y", "z", "x", "c"))
    step, head = ("y", "z"), ("x", "c")
    in_specs = (
        P(step, head, None),
        P(step),
        P(step),
        P(),
        P(),
        P(),
        P(),
        P(None, head),
        P(),
        P(head, None),
        P(),
    )
    out_specs = P(step, head, None)
    return jax.shard_map(local, mesh=grid, in_specs=in_specs, out_specs=out_specs, check_vma=False)
```

```python
import math

import jax
import jax.numpy as jnp
import numpy as np
from jax import lax
from jax.experimental import pallas as pl
from jax.experimental.pallas import tpu as pltpu
from jax.sharding import Mesh
from jax.sharding import PartitionSpec as P

NY, NZ, NX, NC = 4, 8, 4, 2
D = 3072
HD = 128
HL = 3
C = 64
S = 256
ROWS = 32
GRID_W = 16
ROT_DIM = 56
EPS = 1e-06
BF = jnp.bfloat16
F32 = jnp.float32
MIB = 1024 * 1024

VM = pl.BlockSpec(memory_space=pltpu.VMEM)
HB = pl.BlockSpec(memory_space=pltpu.HBM)
SM = pl.BlockSpec(memory_space=pltpu.SMEM)


def pack(x):
    return jnp.concatenate([x[:16], x[16:]], axis=1)


def unpack(x):
    return jnp.concatenate([x[:, :C], x[:, C:]], axis=0)


FREQ = [float(np.float32(10000.0 ** (-j * 2.0 / ROT_DIM))) for j in range(ROT_DIM // 2)]
QKV = 3 * HD


def swap_lanes(x):
    lane = lax.broadcasted_iota(jnp.int32, x.shape, len(x.shape) - 1)
    axis = len(x.shape) - 1
    return jnp.where(lane % 2 == 0, pltpu.roll(x, HD - 1, axis), pltpu.roll(x, 1, axis))


def halves(x):
    high = x.astype(BF)
    return high, (x - high.astype(F32)).astype(BF)


def prepare_kernel(offsets, gain, w_in, mod, tab, wc, rows):
    lane = lax.broadcasted_iota(jnp.int32, (1, HD), 1)
    pair = lane // 2
    by_row = jnp.zeros((1, HD), F32)
    by_col = jnp.zeros((1, HD), F32)
    count = ROT_DIM // 2
    for j in range(count):
        by_row = jnp.where(pair == HD // 2 - 2 * count + j, FREQ[j], by_row)
        by_col = jnp.where(pair == HD // 2 - count + j, FREQ[j], by_col)
    index = lax.broadcasted_iota(jnp.int32, (1, S), 1)
    row = (index // GRID_W + offsets[0:1, :]).astype(F32)
    col = (index % GRID_W + offsets[1:2, :]).astype(F32)
    both = jnp.concatenate([row, col, jnp.zeros((6, S), F32)], axis=0).T
    angle = both[:, 0:1] * by_row + both[:, 1:2] * by_col
    cosine = jnp.cos(angle)
    sine = jnp.sin(angle) * jnp.where(lane % 2 == 0, -1.0, 1.0)
    for k in range(2):
        g = gain[k : k + 1, :]
        turned = swap_lanes(jnp.broadcast_to(g, (8, HD)))[0:1]
        tab[2 * k] = (cosine * g).reshape(8, ROWS, HD)
        tab[2 * k + 1] = (sine * turned).reshape(8, ROWS, HD)
    w = w_in[...].astype(F32)
    w = w - jnp.sum(w, axis=-1, keepdims=True) * (1.0 / D)
    high, low = halves(w)
    wc[:C, :] = high
    wc[C:, :] = low
    rows[0:1, :] = 1.0 + mod[1:2, :]
    rows[1:2, :] = mod[0:1, :]
    rows[2:3, :] = mod[2:3, :]
    rows[3:, :] = jnp.zeros((5, D), F32)


def block_body(chunk_of, wait, cuts, tab, wc, rows, w_qkv, mine, send, zs, es, fs, qkv, qs):
    my_x, my_c = lax.axis_index("x"), lax.axis_index("c")
    order = [((my_x + r % 4) % 4) * 2 + (my_c + r // 4) % 2 for r in range(8)]
    for r in range(8):
        piece = chunk_of(order[r])
        zs[32 * r : 32 * r + 16, :] = piece[:, :C]
        zs[32 * r + 16 : 32 * r + 32, :] = piece[:, C:]
    z = zs[...]
    twice = jnp.concatenate([z, z], axis=1)
    total = jnp.zeros((S, 128), F32)
    wait("wc")
    for j in range(6):
        cut = slice(j * 512, j * 512 + 512)
        e = jnp.dot(twice, wc[:, cut], preferred_element_type=F32)
        es[:, cut] = e
        e = e * e
        total += (e[:, :128] + e[:, 128:256]) + (e[:, 256:384] + e[:, 384:])
    scale = lax.rsqrt(jnp.sum(total, axis=-1, keepdims=True) * (1.0 / D) + EPS)
    wait("rows")
    for j in range(6):
        cut = slice(j * 512, j * 512 + 512)
        fs[:, cut] = (es[:, cut] * scale * rows[0:1, cut] + rows[1:2, cut]).astype(BF)
    for i, (low, high) in enumerate(cuts):
        wait(i)
        qkv[:, low:high] = jnp.dot(fs[...], w_qkv[:, low:high], preferred_element_type=F32)
    wait("tab")
    mean = jnp.full((2 * HD, HD), 1.0 / HD, BF)

    def table(k):
        return jnp.concatenate([tab[k, order[r]] for r in range(8)], axis=0)

    def turned(x, k):
        high, low = halves(x * x)
        square = jnp.dot(jnp.concatenate([high, low], axis=1), mean, preferred_element_type=F32)
        x = x * table(2 * k) + swap_lanes(x) * table(2 * k + 1)
        return (x * lax.rsqrt(square + EPS)).astype(BF)

    for head in range(HL):
        base = head * QKV
        for k in range(2):
            qs[head, k] = turned(qkv[:, base + k * HD : base + k * HD + HD], k)
        qs[head, 2] = qkv[:, base + 2 * HD : base + QKV].astype(BF)
        scores = lax.dot_general(
            qs[head, 0], qs[head, 1], (((1,), (1,)), ((), ())), preferred_element_type=F32
        )
        top = jnp.max(scores, axis=-1, keepdims=True)
        p = jnp.exp((scores - top) * (1.0 / math.sqrt(HD)))
        p = p * (1.0 / jnp.sum(p, axis=-1, keepdims=True))
        out = jnp.dot(p.astype(BF), qs[head, 2], preferred_element_type=F32).astype(BF)
        mine[:, head * HD : head * HD + HD] = out[: S // 2]
        send[:, head * HD : head * HD + HD] = out[S // 2 :]


WHOLE = ((0, HL * QKV),)


def no_wait(key):
    return None


def first_kernel(zg, *rest):
    block_body(lambda i: zg[i], no_wait, WHOLE, *rest)


def second_kernel(zg, parts, tab, wc, rows, w_qkv, mine, send, z_out, *scratch):
    start = lax.axis_index("y") * NZ + lax.axis_index("z") == 0

    def chunk_of(i):
        x, c = i // 2, i % 2
        total = (parts[0, x, c] + parts[1, x, c]) + (parts[2, x, c] + parts[3, x, c])
        return jnp.where(start, zg[i].astype(F32), total).astype(BF)

    z_out[...] = chunk_of(lax.axis_index("x") * 2 + lax.axis_index("c"))
    block_body(chunk_of, no_wait, WHOLE, tab, wc, rows, w_qkv, mine, send, *scratch)


BLOCK_SCRATCH = [
    pltpu.VMEM((S, C), BF),
    pltpu.VMEM((S, D), F32),
    pltpu.VMEM((S, D), BF),
    pltpu.VMEM((S, HL * QKV), F32),
    pltpu.VMEM((HL, 3, S, HD), BF),
]


def projected(mine, peer, w_mine, w_peer, cut):
    middle = jnp.concatenate([mine[:, 2 * HD :], peer[:, :HD]], axis=1)
    w_middle = jnp.concatenate([w_mine[2 * HD :, cut], w_peer[:HD, cut]], axis=0)
    part = jnp.dot(mine[:, : 2 * HD], w_mine[: 2 * HD, cut], preferred_element_type=F32)
    part += jnp.dot(middle, w_middle, preferred_element_type=F32)
    part += jnp.dot(peer[:, HD:], w_peer[HD:, cut], preferred_element_type=F32)
    return part.astype(BF)


def out_kernel(mine, peer, w_mine, w_peer, *outs):
    for j in range(6):
        cut = slice(j * 512, j * 512 + 512)
        part = projected(mine, peer, w_mine, w_peer, cut)
        for k in range(NX):
            outs[k][:, cut] = part[ROWS * k : ROWS * (k + 1)]


def drift_kernel(size, z, zstart, p0, p1, p2, p3, w_in, gate, w_fin, out):
    e = jnp.dot(unpack(z[...]), w_in[...], preferred_element_type=F32)
    attn = p0[...].astype(F32) + p1[...].astype(F32) + p2[...].astype(F32) + p3[...].astype(F32)
    h = e + gate[2:3, :] * attn
    mean = jnp.sum(h, axis=-1, keepdims=True) * (1.0 / D)
    h = h - mean
    var = jnp.sum(h * h, axis=-1, keepdims=True) * (1.0 / D)
    normed = (h * lax.rsqrt(var + EPS)).astype(BF)
    drift = size[0] * lax.dot_general(
        normed, w_fin[...], (((1,), (1,)), ((), ())), preferred_element_type=F32
    )
    start = lax.axis_index("y") * NZ + lax.axis_index("z") == 0
    drift = drift + jnp.where(start, zstart[...], jnp.zeros((ROWS, C), F32))
    packed = pack(drift)
    for k in range(out.shape[0]):
        out[k] = packed


def relay_kernel(got, out):
    y, z = lax.axis_index("y"), lax.axis_index("z")
    for to in range(NY):
        total = jnp.zeros((NC, 16, 128), F32)
        for s in range(NZ):
            keep = y * NZ + s < to * NZ + z
            total = total + jnp.where(keep, got[s], jnp.zeros((NC, 16, 128), F32))
        for x in range(NX):
            out[to, x] = total


def final_kernel(slide, got, out):
    here = lax.axis_index("y") * NZ + lax.axis_index("z")
    target = jnp.minimum(here + slide[0], NY * NZ - 1)
    total = got[0]
    for s in range(1, NY * NZ - 1):
        total = total + jnp.where(s < target, got[s], jnp.zeros((16, 128), F32))
    out[0] = unpack(total)


def call(body, out_shape, in_specs, scratch=(), limit=8):
    several = isinstance(out_shape, (list, tuple))
    return pl.pallas_call(
        body,
        out_shape=out_shape,
        in_specs=in_specs,
        out_specs=[VM] * len(out_shape) if several else VM,
        scratch_shapes=list(scratch),
        compiler_params=pltpu.CompilerParams(vmem_limit_bytes=limit * MIB),
    )


def shape(dims, dtype):
    return jax.ShapeDtypeStruct(dims, dtype)


def swap_cores(x):
    return lax.ppermute(x, "c", [(0, 1), (1, 0)])


def local(
    guesses, step_ids, step_sizes, slide, offsets, mod_table, w_in, w_qkv, qk_gain, w_out, w_fin
):
    state = guesses[0]
    w_peer = swap_cores(w_out)
    z = pack(state.astype(BF))
    zg = lax.all_to_all(jnp.broadcast_to(z[None], (8, 16, 128)), ("x", "c"), 0, 0, tiled=True)
    w_fin_rows = w_fin.T
    mod = lax.dynamic_index_in_dim(mod_table, step_ids[0], 0, keepdims=False)
    tab, wc, rows = call(
        prepare_kernel,
        [shape((4, 8, ROWS, HD), F32), shape((2 * C, D), BF), shape((8, D), F32)],
        [VM] * 4,
        limit=12,
    )(offsets.T, qk_gain, w_in, mod)
    half = shape((S // 2, HL * HD), BF)
    row = shape((ROWS, D), BF)

    def to_right(x, k):
        return lax.ppermute(x, "x", [(i, (i + k) % NX) for i in range(NX)])

    def to_drift(mine, send, z, w_peer, copies):
        operands = (mine, swap_cores(send), w_out, w_peer)
        parts = call(out_kernel, [row] * NX, [VM] * 4, limit=16)(*operands)
        got = [to_right(parts[k], k) for k in (2, 1, 3)]
        return call(drift_kernel, shape((copies, 16, 128), F32), [SM] + [VM] * 9)(
            step_sizes, z, state, parts[0], *got, w_in, rows, w_fin_rows
        )

    mine, send = call(
        first_kernel, [half, half], [VM] * 5, BLOCK_SCRATCH, limit=16
    )(zg, tab, wc, rows, w_qkv)
    drift = to_drift(mine, send, z, w_peer, NZ * NC)
    got = lax.all_to_all(drift, ("z", "c"), 0, 0, tiled=True)
    parts = call(relay_kernel, shape((NY, NX, NC, 16, 128), F32), [VM])(
        got.reshape(NZ, NC, 16, 128)
    )
    parts = lax.all_to_all(
        parts.reshape(NY * NX, NC, 16, 128), ("y", "x"), 0, 0, tiled=True
    ).reshape(NY, NX, NC, 16, 128)
    mine, send, z = call(
        second_kernel,
        [half, half, shape((16, 128), BF)],
        [VM] * 6,
        BLOCK_SCRATCH,
        limit=16,
    )(zg, parts, tab, wc, rows, w_qkv)
    drift = to_drift(mine, send, z, w_peer, NY * NZ)
    got = lax.all_to_all(drift, ("y", "z"), 0, 0, tiled=True)
    return call(final_kernel, shape((1, ROWS, C), F32), [SM, VM])(slide, got)


def solution(mesh):
    grid = Mesh(mesh.devices.reshape(NY, NZ, NX, NC), ("y", "z", "x", "c"))
    step, head = ("y", "z"), ("x", "c")
    in_specs = (
        P(step, head, None),
        P(step),
        P(step),
        P(),
        P(),
        P(),
        P(),
        P(None, head),
        P(),
        P(head, None),
        P(),
    )
    out_specs = P(step, head, None)
    return jax.shard_map(local, mesh=grid, in_specs=in_specs, out_specs=out_specs, check_vma=False)
```

```python
import math

import jax
import jax.numpy as jnp
import numpy as np
from jax import lax
from jax.experimental import pallas as pl
from jax.experimental.pallas import tpu as pltpu
from jax.sharding import Mesh
from jax.sharding import PartitionSpec as P

NY, NZ, NX, NC = 4, 8, 4, 2
D = 3072
HD = 128
HL = 3
C = 64
S = 256
ROWS = 32
GRID_W = 16
ROT_DIM = 56
EPS = 1e-06
BF = jnp.bfloat16
F32 = jnp.float32
MIB = 1024 * 1024

VM = pl.BlockSpec(memory_space=pltpu.VMEM)
HB = pl.BlockSpec(memory_space=pltpu.HBM)
SM = pl.BlockSpec(memory_space=pltpu.SMEM)


def pack(x):
    return jnp.concatenate([x[:16], x[16:]], axis=1)


def unpack(x):
    return jnp.concatenate([x[:, :C], x[:, C:]], axis=0)


FREQ = [float(np.float32(10000.0 ** (-j * 2.0 / ROT_DIM))) for j in range(ROT_DIM // 2)]
QKV = 3 * HD


def swap_lanes(x):
    lane = lax.broadcasted_iota(jnp.int32, x.shape, len(x.shape) - 1)
    axis = len(x.shape) - 1
    return jnp.where(lane % 2 == 0, pltpu.roll(x, HD - 1, axis), pltpu.roll(x, 1, axis))


def halves(x):
    high = x.astype(BF)
    return high, (x - high.astype(F32)).astype(BF)


def prepare_kernel(
    step, after, offsets, gain, w_in, mod_table, w_fin, w_qkv, w_out,
    tab, wc, rows, w_in_out, w_fin_out, w_qkv_out, w_out_out,
    offv, gainv, modv, sems,
):
    at = jnp.clip(step[0], 0, mod_table.shape[1] - 1)
    block = pl.ds(pl.multiple_of(at // 8 * 8, 8), 8)
    pairs = [
        (offsets, offv),
        (gain, gainv),
        (w_in, w_in_out),
        (mod_table.at[:, block, :], modv),
        (w_qkv, w_qkv_out),
        (w_out, w_out_out),
        (w_fin, w_fin_out),
    ]
    copies = [pltpu.make_async_copy(a, b, sems.at[i]) for i, (a, b) in enumerate(pairs)]
    for copy in copies:
        copy.start()
    lane = lax.broadcasted_iota(jnp.int32, (1, HD), 1)
    pair = lane // 2
    by_row = jnp.zeros((1, HD), F32)
    by_col = jnp.zeros((1, HD), F32)
    count = ROT_DIM // 2
    for j in range(count):
        by_row = jnp.where(pair == HD // 2 - 2 * count + j, FREQ[j], by_row)
        by_col = jnp.where(pair == HD // 2 - count + j, FREQ[j], by_col)
    copies[0].wait()
    index = lax.broadcasted_iota(jnp.int32, (1, S), 1)
    row = (index // GRID_W + offv[0:1, :]).astype(F32)
    col = (index % GRID_W + offv[1:2, :]).astype(F32)
    both = jnp.concatenate([row, col, jnp.zeros((6, S), F32)], axis=0).T
    angle = both[:, 0:1] * by_row + both[:, 1:2] * by_col
    cosine = jnp.cos(angle)
    sine = jnp.sin(angle) * jnp.where(lane % 2 == 0, -1.0, 1.0)
    copies[1].wait()
    for k in range(2):
        g = gainv[k : k + 1, :]
        turned = swap_lanes(jnp.broadcast_to(g, (8, HD)))[0:1]
        tab[2 * k] = (cosine * g).reshape(8, ROWS, HD)
        tab[2 * k + 1] = (sine * turned).reshape(8, ROWS, HD)
    copies[2].wait()
    w = w_in_out[...].astype(F32)
    w = w - jnp.sum(w, axis=-1, keepdims=True) * (1.0 / D)
    high, low = halves(w)
    wc[:C, :] = high
    wc[C:, :] = low
    copies[3].wait()
    chosen = lax.broadcasted_iota(jnp.int32, (8, D), 0) == at % 8

    def pick(k):
        return jnp.sum(jnp.where(chosen, modv[k], 0.0), axis=0, keepdims=True)

    rows[0:1, :] = 1.0 + pick(1)
    rows[1:2, :] = pick(0)
    rows[2:3, :] = pick(2)
    rows[3:, :] = jnp.zeros((5, D), F32)
    for copy in copies[4:]:
        copy.wait()


PREPARE_SCRATCH = [
    pltpu.VMEM((2, S), jnp.int32),
    pltpu.VMEM((2, HD), F32),
    pltpu.VMEM((3, 8, D), F32),
    pltpu.SemaphoreType.DMA((7,)),
]


def block_body(chunk_of, tab, wc, rows, w_qkv, mine, send, zs, es, fs, qkv, qs):
    my_x, my_c = lax.axis_index("x"), lax.axis_index("c")
    order = [((my_x + r % 4) % 4) * 2 + (my_c + r // 4) % 2 for r in range(8)]
    for r in range(8):
        piece = chunk_of(r, order[r])
        zs[32 * r : 32 * r + 16, :] = piece[:, :C]
        zs[32 * r + 16 : 32 * r + 32, :] = piece[:, C:]
    z = zs[...]
    twice = jnp.concatenate([z, z], axis=1)
    total = jnp.zeros((S, 128), F32)
    for j in range(6):
        cut = slice(j * 512, j * 512 + 512)
        e = jnp.dot(twice, wc[:, cut], preferred_element_type=F32)
        es[:, cut] = e
        e = e * e
        total += (e[:, :128] + e[:, 128:256]) + (e[:, 256:384] + e[:, 384:])
    scale = lax.rsqrt(jnp.sum(total, axis=-1, keepdims=True) * (1.0 / D) + EPS)
    for j in range(6):
        cut = slice(j * 512, j * 512 + 512)
        fs[:, cut] = (es[:, cut] * scale * rows[0:1, cut] + rows[1:2, cut]).astype(BF)
    qkv[...] = jnp.dot(fs[...], w_qkv[...], preferred_element_type=F32)
    mean = jnp.full((2 * HD, HD), 1.0 / HD, BF)

    def table(k):
        return jnp.concatenate([tab[k, order[r]] for r in range(8)], axis=0)

    def turned(x, k):
        high, low = halves(x * x)
        square = jnp.dot(jnp.concatenate([high, low], axis=1), mean, preferred_element_type=F32)
        x = x * table(2 * k) + swap_lanes(x) * table(2 * k + 1)
        return (x * lax.rsqrt(square + EPS)).astype(BF)

    for head in range(HL):
        base = head * QKV
        for k in range(2):
            qs[head, k] = turned(qkv[:, base + k * HD : base + k * HD + HD], k)
        qs[head, 2] = qkv[:, base + 2 * HD : base + QKV].astype(BF)
        scores = lax.dot_general(
            qs[head, 0], qs[head, 1], (((1,), (1,)), ((), ())), preferred_element_type=F32
        )
        top = jnp.max(scores, axis=-1, keepdims=True)
        p = jnp.exp((scores - top) * (1.0 / math.sqrt(HD)))
        p = p * (1.0 / jnp.sum(p, axis=-1, keepdims=True))
        out = jnp.dot(p.astype(BF), qs[head, 2], preferred_element_type=F32).astype(BF)
        mine[:, head * HD : head * HD + HD] = out[: S // 2]
        send[:, head * HD : head * HD + HD] = out[S // 2 :]


def first_kernel(z0, z1, z2, z3, *rest):
    z = (z0, z1, z2, z3)
    block_body(lambda r, i: z[r % 4][r // 4], *rest)


def second_kernel(
    z0, z1, z2, z3, parts, tab, wc, rows, w_qkv, mine, send, z_out, *scratch
):
    z = (z0, z1, z2, z3)
    start = lax.axis_index("y") * NZ + lax.axis_index("z") == 0

    def chunk_of(r, i):
        x, c = i // 2, i % 2
        total = (parts[0, x, c] + parts[1, x, c]) + (parts[2, x, c] + parts[3, x, c])
        return jnp.where(start, z[r % 4][r // 4].astype(F32), total).astype(BF)

    z_out[...] = chunk_of(0, lax.axis_index("x") * 2 + lax.axis_index("c"))
    block_body(chunk_of, tab, wc, rows, w_qkv, mine, send, *scratch)


BLOCK_SCRATCH = [
    pltpu.VMEM((S, C), BF),
    pltpu.VMEM((S, D), F32),
    pltpu.VMEM((S, D), BF),
    pltpu.VMEM((S, HL * QKV), F32),
    pltpu.VMEM((HL, 3, S, HD), BF),
]


def projected(mine, peer, w_mine, w_peer, cut):
    middle = jnp.concatenate([mine[:, 2 * HD :], peer[:, :HD]], axis=1)
    w_middle = jnp.concatenate([w_mine[2 * HD :, cut], w_peer[:HD, cut]], axis=0)
    part = jnp.dot(mine[:, : 2 * HD], w_mine[: 2 * HD, cut], preferred_element_type=F32)
    part += jnp.dot(middle, w_middle, preferred_element_type=F32)
    part += jnp.dot(peer[:, HD:], w_peer[HD:, cut], preferred_element_type=F32)
    return part.astype(BF)


def out_kernel(mine, peer, w_mine, w_peer, *outs):
    for j in range(6):
        cut = slice(j * 512, j * 512 + 512)
        part = projected(mine, peer, w_mine, w_peer, cut)
        for k in range(NX):
            outs[k][:, cut] = part[ROWS * k : ROWS * (k + 1)]


def drift_kernel(size, z, zstart, p0, p1, p2, p3, w_in, gate, w_fin, out):
    e = jnp.dot(unpack(z[...]), w_in[...], preferred_element_type=F32)
    attn = p0[...].astype(F32) + p1[...].astype(F32) + p2[...].astype(F32) + p3[...].astype(F32)
    h = e + gate[2:3, :] * attn
    mean = jnp.sum(h, axis=-1, keepdims=True) * (1.0 / D)
    h = h - mean
    var = jnp.sum(h * h, axis=-1, keepdims=True) * (1.0 / D)
    normed = (h * lax.rsqrt(var + EPS)).astype(BF)
    drift = size[0] * lax.dot_general(
        normed, w_fin[...], (((1,), (1,)), ((), ())), preferred_element_type=F32
    )
    start = lax.axis_index("y") * NZ + lax.axis_index("z") == 0
    drift = drift + jnp.where(start, zstart[...], jnp.zeros((ROWS, C), F32))
    packed = pack(drift)
    for k in range(out.shape[0]):
        out[k] = packed


def relay_kernel(got, out):
    y, z = lax.axis_index("y"), lax.axis_index("z")
    for to in range(NY):
        total = jnp.zeros((NC, 16, 128), F32)
        for s in range(NZ):
            keep = y * NZ + s < to * NZ + z
            total = total + jnp.where(keep, got[s], jnp.zeros((NC, 16, 128), F32))
        for x in range(NX):
            out[to, x] = total


def final_kernel(slide, got, out):
    here = lax.axis_index("y") * NZ + lax.axis_index("z")
    target = jnp.minimum(here + slide[0], NY * NZ - 1)
    total = got[0]
    for s in range(1, NY * NZ - 1):
        total = total + jnp.where(s < target, got[s], jnp.zeros((16, 128), F32))
    out[0] = unpack(total)


def call(body, out_shape, in_specs, scratch=(), limit=8):
    several = isinstance(out_shape, (list, tuple))
    return pl.pallas_call(
        body,
        out_shape=out_shape,
        in_specs=in_specs,
        out_specs=[VM] * len(out_shape) if several else VM,
        scratch_shapes=list(scratch),
        compiler_params=pltpu.CompilerParams(vmem_limit_bytes=limit * MIB),
    )


def shape(dims, dtype):
    return jax.ShapeDtypeStruct(dims, dtype)


def kept(dims, dtype):
    return pltpu.VMEM(dims, dtype)


def far(x):
    return pltpu.with_memory_space_constraint(x, pltpu.HBM)


def to_right(x, k):
    return lax.ppermute(x, "x", [(i, (i + k) % NX) for i in range(NX)])


def swap_cores(x):
    return lax.ppermute(x, "c", [(0, 1), (1, 0)])


def local(
    guesses, step_ids, step_sizes, slide, offsets, mod_table, w_in, w_qkv, qk_gain, w_out, w_fin
):
    state = guesses[0]
    z = pack(state.astype(BF))
    own = jnp.stack([z, swap_cores(z)])
    w_peer = swap_cores(lax.optimization_barrier((w_out, own))[0])
    zg = [own] + [to_right(own, NX - k) for k in range(1, NX)]
    operands = (offsets.T, qk_gain, w_in, mod_table.transpose(1, 0, 2), w_fin.T, w_qkv, w_out)
    tab, wc, rows, w_in, w_fin_rows, w_qkv, w_out = call(
        prepare_kernel,
        [
            kept((4, 8, ROWS, HD), F32),
            kept((2 * C, D), BF),
            kept((8, D), F32),
            kept((C, D), BF),
            kept((C, D), BF),
            kept(w_qkv.shape, BF),
            kept(w_out.shape, BF),
        ],
        [SM, VM] + [HB] * 7,
        PREPARE_SCRATCH,
        limit=12,
    )(step_ids, own, *[far(x) for x in operands])
    half = shape((S // 2, HL * HD), BF)
    row = shape((ROWS, D), BF)

    def to_drift(mine, send, z, w_peer, copies):
        operands = (mine, swap_cores(send), w_out, w_peer)
        parts = call(out_kernel, [row] * NX, [VM] * 4, limit=16)(*operands)
        got = [to_right(parts[k], k) for k in (2, 1, 3)]
        return call(drift_kernel, shape((copies, 16, 128), F32), [SM] + [VM] * 9)(
            step_sizes, z, state, parts[0], *got, w_in, rows, w_fin_rows
        )

    mine, send = call(first_kernel, [half, half], [VM] * 8, BLOCK_SCRATCH, limit=16)(
        *zg, tab, wc, rows, w_qkv
    )
    drift = to_drift(mine, send, z, w_peer, NZ * NC)
    got = lax.all_to_all(drift, ("z", "c"), 0, 0, tiled=True)
    parts = call(relay_kernel, shape((NY, NX, NC, 16, 128), F32), [VM])(
        got.reshape(NZ, NC, 16, 128)
    )
    parts = lax.all_to_all(
        parts.reshape(NY * NX, NC, 16, 128), ("y", "x"), 0, 0, tiled=True
    ).reshape(NY, NX, NC, 16, 128)
    mine, send, z = call(
        second_kernel,
        [half, half, shape((16, 128), BF)],
        [VM] * 9,
        BLOCK_SCRATCH,
        limit=16,
    )(*zg, parts, tab, wc, rows, w_qkv)
    drift = to_drift(mine, send, z, w_peer, NY * NZ)
    got = lax.all_to_all(drift, ("y", "z"), 0, 0, tiled=True)
    return call(final_kernel, shape((1, ROWS, C), F32), [SM, VM])(slide, got)


def solution(mesh):
    grid = Mesh(mesh.devices.reshape(NY, NZ, NX, NC), ("y", "z", "x", "c"))
    step, head = ("y", "z"), ("x", "c")
    in_specs = (
        P(step, head, None),
        P(step),
        P(step),
        P(),
        P(),
        P(),
        P(),
        P(None, head),
        P(),
        P(head, None),
        P(),
    )
    out_specs = P(step, head, None)
    return jax.shard_map(local, mesh=grid, in_specs=in_specs, out_specs=out_specs, check_vma=False)
```

```python
import math

import jax
import jax.numpy as jnp
import numpy as np
from jax import lax
from jax.experimental import pallas as pl
from jax.experimental.pallas import tpu as pltpu
from jax.sharding import Mesh
from jax.sharding import PartitionSpec as P

NY, NZ, NX, NC = 4, 8, 4, 2
D = 3072
HD = 128
HL = 3
C = 64
S = 256
ROWS = 32
GRID_W = 16
ROT_DIM = 56
EPS = 1e-06
BF = jnp.bfloat16
F32 = jnp.float32
MIB = 1024 * 1024

VM = pl.BlockSpec(memory_space=pltpu.VMEM)
HB = pl.BlockSpec(memory_space=pltpu.HBM)
SM = pl.BlockSpec(memory_space=pltpu.SMEM)


def pack(x):
    return jnp.concatenate([x[:16], x[16:]], axis=1)


def unpack(x):
    return jnp.concatenate([x[:, :C], x[:, C:]], axis=0)


FREQ = [float(np.float32(10000.0 ** (-j * 2.0 / ROT_DIM))) for j in range(ROT_DIM // 2)]
QKV = 3 * HD


def swap_lanes(x):
    lane = lax.broadcasted_iota(jnp.int32, x.shape, len(x.shape) - 1)
    axis = len(x.shape) - 1
    return jnp.where(lane % 2 == 0, pltpu.roll(x, HD - 1, axis), pltpu.roll(x, 1, axis))


def halves(x):
    high = x.astype(BF)
    return high, (x - high.astype(F32)).astype(BF)


def prepare_kernel(
    step, after, offsets, gain, w_in, mod_table, w_fin, w_qkv, w_out,
    tab, wc, rows, w_in_out, w_fin_out, w_qkv_out, w_out_out,
    offv, gainv, modv, sems,
):
    at = jnp.clip(step[0], 0, mod_table.shape[1] - 1)
    block = pl.ds(pl.multiple_of(at // 8 * 8, 8), 8)
    pairs = [
        (offsets, offv),
        (gain, gainv),
        (w_in, w_in_out),
        (mod_table.at[:, block, :], modv),
        (w_qkv, w_qkv_out),
        (w_out, w_out_out),
        (w_fin, w_fin_out),
    ]
    copies = [pltpu.make_async_copy(a, b, sems.at[i]) for i, (a, b) in enumerate(pairs)]
    for copy in copies:
        copy.start()
    lane = lax.broadcasted_iota(jnp.int32, (1, HD), 1)
    pair = lane // 2
    by_row = jnp.zeros((1, HD), F32)
    by_col = jnp.zeros((1, HD), F32)
    count = ROT_DIM // 2
    for j in range(count):
        by_row = jnp.where(pair == HD // 2 - 2 * count + j, FREQ[j], by_row)
        by_col = jnp.where(pair == HD // 2 - count + j, FREQ[j], by_col)
    copies[0].wait()
    index = lax.broadcasted_iota(jnp.int32, (1, S), 1)
    row = (index // GRID_W + offv[0:1, :]).astype(F32)
    col = (index % GRID_W + offv[1:2, :]).astype(F32)
    both = jnp.concatenate([row, col, jnp.zeros((6, S), F32)], axis=0).T
    angle = both[:, 0:1] * by_row + both[:, 1:2] * by_col
    cosine = jnp.cos(angle)
    sine = jnp.sin(angle) * jnp.where(lane % 2 == 0, -1.0, 1.0)
    copies[1].wait()
    for k in range(2):
        g = gainv[k : k + 1, :]
        turned = swap_lanes(jnp.broadcast_to(g, (8, HD)))[0:1]
        tab[2 * k] = (cosine * g).reshape(8, ROWS, HD)
        tab[2 * k + 1] = (sine * turned).reshape(8, ROWS, HD)
    copies[2].wait()
    w = w_in_out[...].astype(F32)
    w = w - jnp.sum(w, axis=-1, keepdims=True) * (1.0 / D)
    high, low = halves(w)
    wc[:C, :] = high
    wc[C:, :] = low
    copies[3].wait()
    chosen = lax.broadcasted_iota(jnp.int32, (8, D), 0) == at % 8

    def pick(k):
        return jnp.sum(jnp.where(chosen, modv[k], 0.0), axis=0, keepdims=True)

    rows[0:1, :] = 1.0 + pick(1)
    rows[1:2, :] = pick(0)
    rows[2:3, :] = pick(2)
    rows[3:, :] = jnp.zeros((5, D), F32)
    for copy in copies[4:]:
        copy.wait()


PREPARE_SCRATCH = [
    pltpu.VMEM((2, S), jnp.int32),
    pltpu.VMEM((2, HD), F32),
    pltpu.VMEM((3, 8, D), F32),
    pltpu.SemaphoreType.DMA((7,)),
]


def block_body(chunk_of, tab, wc, rows, w_qkv, mine, send, zs, es, fs, qkv, qs):
    my_x, my_c = lax.axis_index("x"), lax.axis_index("c")
    order = [((my_x + r % 4) % 4) * 2 + (my_c + r // 4) % 2 for r in range(8)]
    for r in range(8):
        piece = chunk_of(r, order[r])
        zs[32 * r : 32 * r + 16, :] = piece[:, :C]
        zs[32 * r + 16 : 32 * r + 32, :] = piece[:, C:]
    z = zs[...]
    twice = jnp.concatenate([z, z], axis=1)
    total = jnp.zeros((S, 128), F32)
    for j in range(6):
        cut = slice(j * 512, j * 512 + 512)
        e = jnp.dot(twice, wc[:, cut], preferred_element_type=F32)
        es[:, cut] = e
        e = e * e
        total += (e[:, :128] + e[:, 128:256]) + (e[:, 256:384] + e[:, 384:])
    scale = lax.rsqrt(jnp.sum(total, axis=-1, keepdims=True) * (1.0 / D) + EPS)
    for j in range(6):
        cut = slice(j * 512, j * 512 + 512)
        fs[:, cut] = (es[:, cut] * scale * rows[0:1, cut] + rows[1:2, cut]).astype(BF)
    qkv[...] = jnp.dot(fs[...], w_qkv[...], preferred_element_type=F32)
    mean = jnp.full((2 * HD, HD), 1.0 / HD, BF)

    def table(k):
        return jnp.concatenate([tab[k, order[r]] for r in range(8)], axis=0)

    def turned(x, k):
        high, low = halves(x * x)
        square = jnp.dot(jnp.concatenate([high, low], axis=1), mean, preferred_element_type=F32)
        x = x * table(2 * k) + swap_lanes(x) * table(2 * k + 1)
        return (x * lax.rsqrt(square + EPS)).astype(BF)

    for head in range(HL):
        base = head * QKV
        for k in range(2):
            qs[head, k] = turned(qkv[:, base + k * HD : base + k * HD + HD], k)
        qs[head, 2] = qkv[:, base + 2 * HD : base + QKV].astype(BF)
        scores = lax.dot_general(
            qs[head, 0], qs[head, 1], (((1,), (1,)), ((), ())), preferred_element_type=F32
        )
        top = jnp.max(scores, axis=-1, keepdims=True)
        p = jnp.exp((scores - top) * (1.0 / math.sqrt(HD)))
        p = p * (1.0 / jnp.sum(p, axis=-1, keepdims=True))
        out = jnp.dot(p.astype(BF), qs[head, 2], preferred_element_type=F32).astype(BF)
        mine[:, head * HD : head * HD + HD] = out[: S // 2]
        send[:, head * HD : head * HD + HD] = out[S // 2 :]


def first_kernel(z0, z1, z2, z3, *rest):
    z = (z0, z1, z2, z3)
    block_body(lambda r, i: z[r % 4][r // 4], *rest)


def second_kernel(
    z0, z1, z2, z3, parts, tab, wc, rows, w_qkv, mine, send, z_out, *scratch
):
    z = (z0, z1, z2, z3)
    start = position() == 0

    def chunk_of(r, i):
        x, c = i // 2, i % 2
        part = [parts[k, x, c].astype(F32) for k in range(NY)]
        total = (part[0] + part[1]) + (part[2] + part[3])
        return jnp.where(start, z[r % 4][r // 4].astype(F32), total).astype(BF)

    z_out[...] = chunk_of(0, lax.axis_index("x") * 2 + lax.axis_index("c"))
    block_body(chunk_of, tab, wc, rows, w_qkv, mine, send, *scratch)


BLOCK_SCRATCH = [
    pltpu.VMEM((S, C), BF),
    pltpu.VMEM((S, D), F32),
    pltpu.VMEM((S, D), BF),
    pltpu.VMEM((S, HL * QKV), F32),
    pltpu.VMEM((HL, 3, S, HD), BF),
]


def projected(mine, peer, w_mine, w_peer, cut):
    middle = jnp.concatenate([mine[:, 2 * HD :], peer[:, :HD]], axis=1)
    w_middle = jnp.concatenate([w_mine[2 * HD :, cut], w_peer[:HD, cut]], axis=0)
    part = jnp.dot(mine[:, : 2 * HD], w_mine[: 2 * HD, cut], preferred_element_type=F32)
    part += jnp.dot(middle, w_middle, preferred_element_type=F32)
    part += jnp.dot(peer[:, HD:], w_peer[HD:, cut], preferred_element_type=F32)
    return part.astype(BF)


def out_kernel(mine, peer, w_mine, w_peer, *outs):
    for j in range(6):
        cut = slice(j * 512, j * 512 + 512)
        part = projected(mine, peer, w_mine, w_peer, cut)
        for k in range(NX):
            outs[k][:, cut] = part[ROWS * k : ROWS * (k + 1)]


def drift(size, z, p0, p1, p2, p3, w_in, gate, w_fin):
    e = jnp.dot(unpack(z[...]), w_in[...], preferred_element_type=F32)
    attn = p0[...].astype(F32) + p1[...].astype(F32) + p2[...].astype(F32) + p3[...].astype(F32)
    h = e + gate[2:3, :] * attn
    mean = jnp.sum(h, axis=-1, keepdims=True) * (1.0 / D)
    h = h - mean
    var = jnp.sum(h * h, axis=-1, keepdims=True) * (1.0 / D)
    normed = (h * lax.rsqrt(var + EPS)).astype(BF)
    return size[0] * lax.dot_general(
        normed, w_fin[...], (((1,), (1,)), ((), ())), preferred_element_type=F32
    )


def position():
    return lax.axis_index("y") * NZ + lax.axis_index("z")


def first_drift_kernel(zstart, *rest):
    out, start = rest[-2:]
    value = drift(*rest[:-2])
    value = value + jnp.where(position() == 0, zstart[...], jnp.zeros((ROWS, C), F32))
    packed = pack(value)
    start[...] = packed
    for k in range(out.shape[0]):
        out[k] = packed.astype(BF)


def second_drift_kernel(start, first, *rest):
    out = rest[-1]
    low = first[...] - first[...].astype(BF).astype(F32)
    here = position()
    value = jnp.where(here == 0, start[...], pack(drift(*rest[:-1])))
    value = jnp.where(here == NY * NZ - 1, low, value).astype(BF)
    for k in range(out.shape[0]):
        out[k] = value


def relay_kernel(got, out):
    y, z = lax.axis_index("y"), lax.axis_index("z")
    for to in range(NY):
        total = jnp.zeros((NC, 16, 128), F32)
        for s in range(NZ):
            keep = y * NZ + s < to * NZ + z
            total = total + jnp.where(keep, got[s].astype(F32), jnp.zeros((NC, 16, 128), F32))
        for x in range(NX):
            out[to, x] = total.astype(out.dtype)


def final_kernel(slide, got, out):
    last = NY * NZ - 1
    target = jnp.minimum(position() + slide[0], last)
    total = got[0].astype(F32) + got[last].astype(F32)
    for s in range(1, last):
        total = total + jnp.where(s < target, got[s].astype(F32), jnp.zeros((16, 128), F32))
    out[0] = unpack(total)


def call(body, out_shape, in_specs, scratch=(), limit=8):
    several = isinstance(out_shape, (list, tuple))
    return pl.pallas_call(
        body,
        out_shape=out_shape,
        in_specs=in_specs,
        out_specs=[VM] * len(out_shape) if several else VM,
        scratch_shapes=list(scratch),
        compiler_params=pltpu.CompilerParams(vmem_limit_bytes=limit * MIB),
    )


def shape(dims, dtype):
    return jax.ShapeDtypeStruct(dims, dtype)


def kept(dims, dtype):
    return pltpu.VMEM(dims, dtype)


def far(x):
    return pltpu.with_memory_space_constraint(x, pltpu.HBM)


def to_right(x, k):
    return lax.ppermute(x, "x", [(i, (i + k) % NX) for i in range(NX)])


def swap_cores(x):
    return lax.ppermute(x, "c", [(0, 1), (1, 0)])


def local(
    guesses, step_ids, step_sizes, slide, offsets, mod_table, w_in, w_qkv, qk_gain, w_out, w_fin
):
    state = guesses[0]
    z = pack(state.astype(BF))
    own = jnp.stack([z, swap_cores(z)])
    w_peer = swap_cores(lax.optimization_barrier((w_out, own))[0])
    zg = [own] + [to_right(own, NX - k) for k in range(1, NX)]
    operands = (offsets.T, qk_gain, w_in, mod_table.transpose(1, 0, 2), w_fin.T, w_qkv, w_out)
    tab, wc, rows, w_in, w_fin_rows, w_qkv, w_out = call(
        prepare_kernel,
        [
            kept((4, 8, ROWS, HD), F32),
            kept((2 * C, D), BF),
            kept((8, D), F32),
            kept((C, D), BF),
            kept((C, D), BF),
            kept(w_qkv.shape, BF),
            kept(w_out.shape, BF),
        ],
        [SM, VM] + [HB] * 7,
        PREPARE_SCRATCH,
        limit=12,
    )(step_ids, own, *[far(x) for x in operands])
    half = shape((S // 2, HL * HD), BF)
    row = shape((ROWS, D), BF)

    def exchanged(mine, send):
        operands = (mine, swap_cores(send), w_out, w_peer)
        parts = call(out_kernel, [row] * NX, [VM] * 4, limit=16)(*operands)
        return [parts[0]] + [to_right(parts[k], k) for k in (2, 1, 3)]

    mine, send = call(first_kernel, [half, half], [VM] * 8, BLOCK_SCRATCH, limit=16)(
        *zg, tab, wc, rows, w_qkv
    )
    outs, start = call(
        first_drift_kernel,
        [shape((NZ * NC, 16, 128), BF), shape((16, 128), F32)],
        [VM, SM] + [VM] * 8,
    )(state, step_sizes, z, *exchanged(mine, send), w_in, rows, w_fin_rows)
    first = lax.ppermute(start, ("y", "z"), [(0, NY * NZ - 1)])
    got = lax.all_to_all(outs, ("z", "c"), 0, 0, tiled=True)
    parts = call(relay_kernel, shape((NY, NX, NC, 16, 128), BF), [VM])(
        got.reshape(NZ, NC, 16, 128)
    )
    parts = lax.all_to_all(
        parts.reshape(NY * NX, NC, 16, 128), ("y", "x"), 0, 0, tiled=True
    ).reshape(NY, NX, NC, 16, 128)
    mine, send, z = call(
        second_kernel,
        [half, half, shape((16, 128), BF)],
        [VM] * 9,
        BLOCK_SCRATCH,
        limit=16,
    )(*zg, parts, tab, wc, rows, w_qkv)
    outs = call(
        second_drift_kernel,
        shape((NY * NZ, 16, 128), BF),
        [VM, VM, SM] + [VM] * 8,
    )(start, first, step_sizes, z, *exchanged(mine, send), w_in, rows, w_fin_rows)
    got = lax.all_to_all(outs, ("y", "z"), 0, 0, tiled=True)
    return call(final_kernel, shape((1, ROWS, C), F32), [SM, VM])(slide, got)


def solution(mesh):
    grid = Mesh(mesh.devices.reshape(NY, NZ, NX, NC), ("y", "z", "x", "c"))
    step, head = ("y", "z"), ("x", "c")
    in_specs = (
        P(step, head, None),
        P(step),
        P(step),
        P(),
        P(),
        P(),
        P(),
        P(None, head),
        P(),
        P(head, None),
        P(),
    )
    out_specs = P(step, head, None)
    return jax.shard_map(local, mesh=grid, in_specs=in_specs, out_specs=out_specs, check_vma=False)
```

```python
import math

import jax
import jax.numpy as jnp
import numpy as np
from jax import lax
from jax.experimental import pallas as pl
from jax.experimental.pallas import tpu as pltpu
from jax.sharding import Mesh
from jax.sharding import PartitionSpec as P

NY, NZ, NX, NC = 4, 8, 4, 2
D = 3072
HD = 128
HL = 3
C = 64
S = 256
ROWS = 32
GRID_W = 16
ROT_DIM = 56
EPS = 1e-06
BF = jnp.bfloat16
F32 = jnp.float32
MIB = 1024 * 1024

VM = pl.BlockSpec(memory_space=pltpu.VMEM)
HB = pl.BlockSpec(memory_space=pltpu.HBM)
SM = pl.BlockSpec(memory_space=pltpu.SMEM)


def pack(x):
    return jnp.concatenate([x[:16], x[16:]], axis=1)


def unpack(x):
    return jnp.concatenate([x[:, :C], x[:, C:]], axis=0)


FREQ = [float(np.float32(10000.0 ** (-j * 2.0 / ROT_DIM))) for j in range(ROT_DIM // 2)]
QKV = 3 * HD


def swap_lanes(x):
    lane = lax.broadcasted_iota(jnp.int32, x.shape, len(x.shape) - 1)
    axis = len(x.shape) - 1
    return jnp.where(lane % 2 == 0, pltpu.roll(x, HD - 1, axis), pltpu.roll(x, 1, axis))


def halves(x):
    high = x.astype(BF)
    return high, (x - high.astype(F32)).astype(BF)


def prepare_kernel(
    step, after, offsets, gain, w_in, mod_table, w_fin, w_qkv, w_out, state,
    tab, wc, rows, w_in_out, w_fin_out, w_qkv_out, w_out_out, state_out,
    offv, gainv, modv, sems,
):
    at = jnp.clip(step[0], 0, mod_table.shape[1] - 1)
    block = pl.ds(pl.multiple_of(at // 8 * 8, 8), 8)
    pairs = [
        (offsets, offv),
        (gain, gainv),
        (w_in, w_in_out),
        (mod_table.at[:, block, :], modv),
        (w_qkv, w_qkv_out),
        (w_out, w_out_out),
        (w_fin, w_fin_out),
        (state, state_out),
    ]
    copies = [pltpu.make_async_copy(a, b, sems.at[i]) for i, (a, b) in enumerate(pairs)]
    for copy in copies:
        copy.start()
    lane = lax.broadcasted_iota(jnp.int32, (1, HD), 1)
    pair = lane // 2
    by_row = jnp.zeros((1, HD), F32)
    by_col = jnp.zeros((1, HD), F32)
    count = ROT_DIM // 2
    for j in range(count):
        by_row = jnp.where(pair == HD // 2 - 2 * count + j, FREQ[j], by_row)
        by_col = jnp.where(pair == HD // 2 - count + j, FREQ[j], by_col)
    copies[0].wait()
    index = lax.broadcasted_iota(jnp.int32, (1, S), 1)
    row = (index // GRID_W + offv[0:1, :]).astype(F32)
    col = (index % GRID_W + offv[1:2, :]).astype(F32)
    both = jnp.concatenate([row, col, jnp.zeros((6, S), F32)], axis=0).T
    angle = both[:, 0:1] * by_row + both[:, 1:2] * by_col
    cosine = jnp.cos(angle)
    sine = jnp.sin(angle) * jnp.where(lane % 2 == 0, -1.0, 1.0)
    copies[1].wait()
    for k in range(2):
        g = gainv[k : k + 1, :]
        turned = swap_lanes(jnp.broadcast_to(g, (8, HD)))[0:1]
        tab[2 * k] = (cosine * g).reshape(8, ROWS, HD)
        tab[2 * k + 1] = (sine * turned).reshape(8, ROWS, HD)
    copies[2].wait()
    w = w_in_out[...].astype(F32)
    w = w - jnp.sum(w, axis=-1, keepdims=True) * (1.0 / D)
    high, low = halves(w)
    wc[:C, :] = high
    wc[C:, :] = low
    copies[3].wait()
    chosen = lax.broadcasted_iota(jnp.int32, (8, D), 0) == at % 8

    def pick(k):
        return jnp.sum(jnp.where(chosen, modv[k], 0.0), axis=0, keepdims=True)

    rows[0:1, :] = 1.0 + pick(1)
    rows[1:2, :] = pick(0)
    rows[2:3, :] = pick(2)
    rows[3:, :] = jnp.zeros((5, D), F32)
    for copy in copies[4:]:
        copy.wait()


PREPARE_SCRATCH = [
    pltpu.VMEM((2, S), jnp.int32),
    pltpu.VMEM((2, HD), F32),
    pltpu.VMEM((3, 8, D), F32),
    pltpu.SemaphoreType.DMA((8,)),
]


def block_body(chunk_of, tab, wc, rows, w_qkv, mine, send, zs, es, fs, qkv, qs):
    my_x, my_c = lax.axis_index("x"), lax.axis_index("c")
    order = [((my_x + r % 4) % 4) * 2 + (my_c + r // 4) % 2 for r in range(8)]
    for r in range(8):
        piece = chunk_of(r, order[r])
        zs[32 * r : 32 * r + 16, :] = piece[:, :C]
        zs[32 * r + 16 : 32 * r + 32, :] = piece[:, C:]
    z = zs[...]
    twice = jnp.concatenate([z, z], axis=1)
    total = jnp.zeros((S, 128), F32)
    for j in range(6):
        cut = slice(j * 512, j * 512 + 512)
        e = jnp.dot(twice, wc[:, cut], preferred_element_type=F32)
        es[:, cut] = e
        e = e * e
        total += (e[:, :128] + e[:, 128:256]) + (e[:, 256:384] + e[:, 384:])
    scale = lax.rsqrt(jnp.sum(total, axis=-1, keepdims=True) * (1.0 / D) + EPS)
    for j in range(6):
        cut = slice(j * 512, j * 512 + 512)
        fs[:, cut] = (es[:, cut] * scale * rows[0:1, cut] + rows[1:2, cut]).astype(BF)
    qkv[...] = jnp.dot(fs[...], w_qkv[...], preferred_element_type=F32)
    mean = jnp.full((2 * HD, HD), 1.0 / HD, BF)

    def table(k):
        return jnp.concatenate([tab[k, order[r]] for r in range(8)], axis=0)

    def turned(x, k):
        high, low = halves(x * x)
        square = jnp.dot(jnp.concatenate([high, low], axis=1), mean, preferred_element_type=F32)
        x = x * table(2 * k) + swap_lanes(x) * table(2 * k + 1)
        return (x * lax.rsqrt(square + EPS)).astype(BF)

    for head in range(HL):
        base = head * QKV
        for k in range(2):
            qs[head, k] = turned(qkv[:, base + k * HD : base + k * HD + HD], k)
        qs[head, 2] = qkv[:, base + 2 * HD : base + QKV].astype(BF)
        scores = lax.dot_general(
            qs[head, 0], qs[head, 1], (((1,), (1,)), ((), ())), preferred_element_type=F32
        )
        top = jnp.max(scores, axis=-1, keepdims=True)
        p = jnp.exp((scores - top) * (1.0 / math.sqrt(HD)))
        p = p * (1.0 / jnp.sum(p, axis=-1, keepdims=True))
        out = jnp.dot(p.astype(BF), qs[head, 2], preferred_element_type=F32).astype(BF)
        mine[:, head * HD : head * HD + HD] = out[: S // 2]
        send[:, head * HD : head * HD + HD] = out[S // 2 :]


def first_kernel(z0, z1, z2, z3, *rest):
    z = (z0, z1, z2, z3)
    block_body(lambda r, i: z[r % 4][r // 4], *rest)


def second_kernel(zg, *rest):
    block_body(lambda r, i: zg[i], *rest)


BLOCK_SCRATCH = [
    pltpu.VMEM((S, C), BF),
    pltpu.VMEM((S, D), F32),
    pltpu.VMEM((S, D), BF),
    pltpu.VMEM((S, HL * QKV), F32),
    pltpu.VMEM((HL, 3, S, HD), BF),
]


def projected(mine, peer, w_mine, w_peer, cut):
    middle = jnp.concatenate([mine[:, 2 * HD :], peer[:, :HD]], axis=1)
    w_middle = jnp.concatenate([w_mine[2 * HD :, cut], w_peer[:HD, cut]], axis=0)
    part = jnp.dot(mine[:, : 2 * HD], w_mine[: 2 * HD, cut], preferred_element_type=F32)
    part += jnp.dot(middle, w_middle, preferred_element_type=F32)
    part += jnp.dot(peer[:, HD:], w_peer[HD:, cut], preferred_element_type=F32)
    return part.astype(BF)


def out_kernel(mine, peer, w_mine, w_peer, *outs):
    for j in range(6):
        cut = slice(j * 512, j * 512 + 512)
        part = projected(mine, peer, w_mine, w_peer, cut)
        for k in range(NX):
            outs[k][:, cut] = part[ROWS * k : ROWS * (k + 1)]


def position():
    return lax.axis_index("y") * NZ + lax.axis_index("z")


LAST = NY * NZ - 1


def drift_kernel(
    size, slide, high, zstart, z, p0, p1, p2, p3, w_in, gate, w_fin, out, target=None
):
    e = jnp.dot(unpack(z[...]), w_in[...], preferred_element_type=F32)
    attn = p0[...].astype(F32) + p1[...].astype(F32) + p2[...].astype(F32) + p3[...].astype(F32)
    h = e + gate[2:3, :] * attn
    mean = jnp.sum(h, axis=-1, keepdims=True) * (1.0 / D)
    h = h - mean
    var = jnp.sum(h * h, axis=-1, keepdims=True) * (1.0 / D)
    normed = (h * lax.rsqrt(var + EPS)).astype(BF)
    drift = size[0] * lax.dot_general(
        normed, w_fin[...], (((1,), (1,)), ((), ())), preferred_element_type=F32
    )
    here = position()
    low = zstart[...] - zstart[...].astype(BF).astype(F32)
    value = pack(drift + jnp.where(here == 0, low, 0.0)).astype(BF)
    value = jnp.where(here == LAST, high[...].astype(F32), value.astype(F32)).astype(BF)
    for k in range(out.shape[0]):
        out[k] = value
    if target is not None:
        target[...] = jnp.full((8, 128), jnp.minimum(here + slide[0], LAST), jnp.int32)


def summed(got, target):
    total = got[0].astype(F32) + got[LAST].astype(F32)
    for s in range(1, LAST):
        total = total + jnp.where(s < target, got[s].astype(F32), 0.0)
    return total


def state_kernel(z, got, z_out, copies):
    here = position()
    value = jnp.where(here == 0, z[...].astype(F32), summed(got, here)).astype(BF)
    z_out[...] = value
    for k in range(8):
        copies[k] = value


def final_kernel(target, got, out):
    out[0] = unpack(summed(got, jnp.concatenate([target[...], target[...]], axis=0)))


def call(body, out_shape, in_specs, scratch=(), limit=8):
    several = isinstance(out_shape, (list, tuple))
    return pl.pallas_call(
        body,
        out_shape=out_shape,
        in_specs=in_specs,
        out_specs=[VM] * len(out_shape) if several else VM,
        scratch_shapes=list(scratch),
        compiler_params=pltpu.CompilerParams(vmem_limit_bytes=limit * MIB),
    )


def shape(dims, dtype):
    return jax.ShapeDtypeStruct(dims, dtype)


def kept(dims, dtype):
    return pltpu.VMEM(dims, dtype)


def far(x):
    return pltpu.with_memory_space_constraint(x, pltpu.HBM)


def to_right(x, k):
    return lax.ppermute(x, "x", [(i, (i + k) % NX) for i in range(NX)])


def swap_cores(x):
    return lax.ppermute(x, "c", [(0, 1), (1, 0)])


def local(
    guesses, step_ids, step_sizes, slide, offsets, mod_table, w_in, w_qkv, qk_gain, w_out, w_fin
):
    state = guesses[0]
    z = pack(state.astype(BF))
    own = jnp.stack([z, swap_cores(z)])
    w_peer = swap_cores(lax.optimization_barrier((w_out, own))[0])
    zg = [own] + [to_right(own, NX - k) for k in range(1, NX)]
    operands = (offsets.T, qk_gain, w_in, mod_table.transpose(1, 0, 2), w_fin.T, w_qkv, w_out)
    operands += (state,)
    tab, wc, rows, w_in, w_fin_rows, w_qkv, w_out, state = call(
        prepare_kernel,
        [
            kept((4, 8, ROWS, HD), F32),
            kept((2 * C, D), BF),
            kept((8, D), F32),
            kept((C, D), BF),
            kept((C, D), BF),
            kept(w_qkv.shape, BF),
            kept(w_out.shape, BF),
            kept((ROWS, C), F32),
        ],
        [SM, VM] + [HB] * 8,
        PREPARE_SCRATCH,
        limit=12,
    )(step_ids, own, *[far(x) for x in operands])
    half = shape((S // 2, HL * HD), BF)
    row = shape((ROWS, D), BF)

    high = lax.ppermute(z, ("y", "z"), [(0, LAST)])

    def gathered_drifts(mine, send, z, *extra):
        operands = (mine, swap_cores(send), w_out, w_peer)
        parts = call(out_kernel, [row] * NX, [VM] * 4, limit=16)(*operands)
        got = [parts[0]] + [to_right(parts[k], k) for k in (2, 1, 3)]
        outs, *extra = call(
            drift_kernel,
            [shape((NY * NZ, 16, 128), BF), *extra],
            [SM, SM] + [VM] * 10,
        )(step_sizes, slide, high, state, z, *got, w_in, rows, w_fin_rows)
        return lax.all_to_all(outs, ("y", "z"), 0, 0, tiled=True), *extra

    mine, send = call(first_kernel, [half, half], [VM] * 8, BLOCK_SCRATCH, limit=16)(
        *zg, tab, wc, rows, w_qkv
    )
    (got,) = gathered_drifts(mine, send, z)
    z, copies = call(
        state_kernel, [shape((16, 128), BF), shape((8, 16, 128), BF)], [VM] * 2
    )(z, got)
    zg = lax.all_to_all(copies, ("x", "c"), 0, 0, tiled=True)
    mine, send = call(second_kernel, [half, half], [VM] * 5, BLOCK_SCRATCH, limit=16)(
        zg, tab, wc, rows, w_qkv
    )
    got, target = gathered_drifts(mine, send, z, shape((8, 128), jnp.int32))
    return call(final_kernel, shape((1, ROWS, C), F32), [VM] * 2)(target, got)


def solution(mesh):
    grid = Mesh(mesh.devices.reshape(NY, NZ, NX, NC), ("y", "z", "x", "c"))
    step, head = ("y", "z"), ("x", "c")
    in_specs = (
        P(step, head, None),
        P(step),
        P(step),
        P(),
        P(),
        P(),
        P(),
        P(None, head),
        P(),
        P(head, None),
        P(),
    )
    out_specs = P(step, head, None)
    return jax.shard_map(local, mesh=grid, in_specs=in_specs, out_specs=out_specs, check_vma=False)
```

```python
import math

import jax
import jax.numpy as jnp
import numpy as np
from jax import lax
from jax.experimental import pallas as pl
from jax.experimental.pallas import tpu as pltpu
from jax.sharding import Mesh
from jax.sharding import PartitionSpec as P

NY, NZ, NX, NC = 4, 8, 4, 2
D = 3072
HD = 128
HL = 3
C = 64
S = 256
ROWS = 32
GRID_W = 16
ROT_DIM = 56
EPS = 1e-06
BF = jnp.bfloat16
F32 = jnp.float32
MIB = 1024 * 1024

VM = pl.BlockSpec(memory_space=pltpu.VMEM)
HB = pl.BlockSpec(memory_space=pltpu.HBM)
SM = pl.BlockSpec(memory_space=pltpu.SMEM)


def pack(x):
    return jnp.concatenate([x[:16], x[16:]], axis=1)


def unpack(x):
    return jnp.concatenate([x[:, :C], x[:, C:]], axis=0)


FREQ = [float(np.float32(10000.0 ** (-j * 2.0 / ROT_DIM))) for j in range(ROT_DIM // 2)]
QKV = 3 * HD


def swap_lanes(x):
    lane = lax.broadcasted_iota(jnp.int32, x.shape, len(x.shape) - 1)
    axis = len(x.shape) - 1
    return jnp.where(lane % 2 == 0, pltpu.roll(x, HD - 1, axis), pltpu.roll(x, 1, axis))


def halves(x):
    high = x.astype(BF)
    return high, (x - high.astype(F32)).astype(BF)


def prepare_kernel(
    step, after, offsets, gain, w_in, mod_table, w_qkv,
    tab, wc, rows, w_in_out, w_qkv_out,
    offv, gainv, modv, sems,
):
    at = jnp.clip(step[0], 0, mod_table.shape[1] - 1)
    block = pl.ds(pl.multiple_of(at // 8 * 8, 8), 8)
    pairs = [
        (offsets, offv),
        (gain, gainv),
        (w_in, w_in_out),
        (mod_table.at[:, block, :], modv),
        (w_qkv, w_qkv_out),
    ]
    copies = [pltpu.make_async_copy(a, b, sems.at[i]) for i, (a, b) in enumerate(pairs)]
    for copy in copies:
        copy.start()
    lane = lax.broadcasted_iota(jnp.int32, (1, HD), 1)
    pair = lane // 2
    by_row = jnp.zeros((1, HD), F32)
    by_col = jnp.zeros((1, HD), F32)
    count = ROT_DIM // 2
    for j in range(count):
        by_row = jnp.where(pair == HD // 2 - 2 * count + j, FREQ[j], by_row)
        by_col = jnp.where(pair == HD // 2 - count + j, FREQ[j], by_col)
    copies[0].wait()
    index = lax.broadcasted_iota(jnp.int32, (1, S), 1)
    row = (index // GRID_W + offv[0:1, :]).astype(F32)
    col = (index % GRID_W + offv[1:2, :]).astype(F32)
    both = jnp.concatenate([row, col, jnp.zeros((6, S), F32)], axis=0).T
    angle = both[:, 0:1] * by_row + both[:, 1:2] * by_col
    cosine = jnp.cos(angle)
    sine = jnp.sin(angle) * jnp.where(lane % 2 == 0, -1.0, 1.0)
    copies[1].wait()
    for k in range(2):
        g = gainv[k : k + 1, :]
        turned = swap_lanes(jnp.broadcast_to(g, (8, HD)))[0:1]
        tab[2 * k] = (cosine * g).reshape(8, ROWS, HD)
        tab[2 * k + 1] = (sine * turned).reshape(8, ROWS, HD)
    copies[2].wait()
    w = w_in_out[...].astype(F32)
    w = w - jnp.sum(w, axis=-1, keepdims=True) * (1.0 / D)
    high, low = halves(w)
    wc[:C, :] = high
    wc[C:, :] = low
    copies[3].wait()
    chosen = lax.broadcasted_iota(jnp.int32, (8, D), 0) == at % 8

    def pick(k):
        return jnp.sum(jnp.where(chosen, modv[k], 0.0), axis=0, keepdims=True)

    rows[0:1, :] = 1.0 + pick(1)
    rows[1:2, :] = pick(0)
    rows[2:3, :] = pick(2)
    rows[3:, :] = jnp.zeros((5, D), F32)
    for copy in copies[4:]:
        copy.wait()


PREPARE_SCRATCH = [
    pltpu.VMEM((2, S), jnp.int32),
    pltpu.VMEM((2, HD), F32),
    pltpu.VMEM((3, 8, D), F32),
    pltpu.SemaphoreType.DMA((5,)),
]


def late_kernel(after, *refs):
    count = len(refs) // 2
    sems = refs[-1]
    copies = [
        pltpu.make_async_copy(refs[i], refs[count + i], sems.at[i]) for i in range(count)
    ]
    for copy in copies:
        copy.start()
    for copy in copies:
        copy.wait()


def block_body(chunk_of, tab, wc, rows, w_qkv, mine, send, zs, es, fs, qkv, qs):
    my_x, my_c = lax.axis_index("x"), lax.axis_index("c")
    order = [((my_x + r % 4) % 4) * 2 + (my_c + r // 4) % 2 for r in range(8)]
    for r in range(8):
        piece = chunk_of(r, order[r])
        zs[32 * r : 32 * r + 16, :] = piece[:, :C]
        zs[32 * r + 16 : 32 * r + 32, :] = piece[:, C:]
    z = zs[...]
    twice = jnp.concatenate([z, z], axis=1)
    total = jnp.zeros((S, 128), F32)
    for j in range(6):
        cut = slice(j * 512, j * 512 + 512)
        e = jnp.dot(twice, wc[:, cut], preferred_element_type=F32)
        es[:, cut] = e
        e = e * e
        total += (e[:, :128] + e[:, 128:256]) + (e[:, 256:384] + e[:, 384:])
    scale = lax.rsqrt(jnp.sum(total, axis=-1, keepdims=True) * (1.0 / D) + EPS)
    for j in range(6):
        cut = slice(j * 512, j * 512 + 512)
        fs[:, cut] = (es[:, cut] * scale * rows[0:1, cut] + rows[1:2, cut]).astype(BF)
    qkv[...] = jnp.dot(fs[...], w_qkv[...], preferred_element_type=F32)
    mean = jnp.full((2 * HD, HD), 1.0 / HD, BF)

    def table(k):
        return jnp.concatenate([tab[k, order[r]] for r in range(8)], axis=0)

    def turned(x, k):
        high, low = halves(x * x)
        square = jnp.dot(jnp.concatenate([high, low], axis=1), mean, preferred_element_type=F32)
        x = x * table(2 * k) + swap_lanes(x) * table(2 * k + 1)
        return (x * lax.rsqrt(square + EPS)).astype(BF)

    for head in range(HL):
        base = head * QKV
        for k in range(2):
            qs[head, k] = turned(qkv[:, base + k * HD : base + k * HD + HD], k)
        qs[head, 2] = qkv[:, base + 2 * HD : base + QKV].astype(BF)
    scores = [
        lax.dot_general(
            qs[head, 0], qs[head, 1], (((1,), (1,)), ((), ())), preferred_element_type=F32
        )
        for head in range(HL)
    ]
    tops = [jnp.max(score, axis=-1, keepdims=True) for score in scores]
    factor = math.log2(math.e) / math.sqrt(HD)
    probs = [jnp.exp2((score - top) * factor) for score, top in zip(scores, tops)]
    totals = [jnp.sum(p, axis=-1, keepdims=True) for p in probs]
    outs = [
        jnp.dot(p.astype(BF), qs[head, 2], preferred_element_type=F32)
        for head, p in enumerate(probs)
    ]
    for head in range(HL):
        out = (outs[head] * (1.0 / totals[head])).astype(BF)
        mine[:, head * HD : head * HD + HD] = out[: S // 2]
        send[:, head * HD : head * HD + HD] = out[S // 2 :]


def first_kernel(z0, z1, z2, z3, *rest):
    z = (z0, z1, z2, z3)
    block_body(lambda r, i: z[r % 4][r // 4], *rest)


def second_kernel(zg, *rest):
    block_body(lambda r, i: zg[i], *rest)


BLOCK_SCRATCH = [
    pltpu.VMEM((S, C), BF),
    pltpu.VMEM((S, D), F32),
    pltpu.VMEM((S, D), BF),
    pltpu.VMEM((S, HL * QKV), F32),
    pltpu.VMEM((HL, 3, S, HD), BF),
]


def projected(mine, peer, w_mine, w_peer, cut):
    middle = jnp.concatenate([mine[:, 2 * HD :], peer[:, :HD]], axis=1)
    w_middle = jnp.concatenate([w_mine[2 * HD :, cut], w_peer[:HD, cut]], axis=0)
    part = jnp.dot(mine[:, : 2 * HD], w_mine[: 2 * HD, cut], preferred_element_type=F32)
    part += jnp.dot(middle, w_middle, preferred_element_type=F32)
    part += jnp.dot(peer[:, HD:], w_peer[HD:, cut], preferred_element_type=F32)
    return part.astype(BF)


def out_kernel(mine, peer, w_mine, w_peer, *outs):
    for j in range(6):
        cut = slice(j * 512, j * 512 + 512)
        part = projected(mine, peer, w_mine, w_peer, cut)
        for k in range(NX):
            outs[k][:, cut] = part[ROWS * k : ROWS * (k + 1)]


def position():
    return lax.axis_index("y") * NZ + lax.axis_index("z")


LAST = NY * NZ - 1


def drift_kernel(
    size, slide, high, zstart, z, p0, p1, p2, p3, w_in, gate, w_fin, out, target=None
):
    e = jnp.dot(unpack(z[...]), w_in[...], preferred_element_type=F32)
    attn = p0[...].astype(F32) + p1[...].astype(F32) + p2[...].astype(F32) + p3[...].astype(F32)
    h = e + gate[2:3, :] * attn
    mean = jnp.sum(h, axis=-1, keepdims=True) * (1.0 / D)
    h = h - mean
    var = jnp.sum(h * h, axis=-1, keepdims=True) * (1.0 / D)
    normed = (h * lax.rsqrt(var + EPS)).astype(BF)
    drift = size[0] * lax.dot_general(
        normed, w_fin[...], (((1,), (1,)), ((), ())), preferred_element_type=F32
    )
    here = position()
    low = zstart[...] - zstart[...].astype(BF).astype(F32)
    value = pack(drift + jnp.where(here == 0, low, 0.0)).astype(BF)
    value = jnp.where(here == LAST, high[...].astype(F32), value.astype(F32)).astype(BF)
    for k in range(out.shape[0]):
        out[k] = value
    if target is not None:
        target[...] = jnp.full((8, 128), jnp.minimum(here + slide[0], LAST), jnp.int32)


def summed(got, target):
    total = got[0].astype(F32) + got[LAST].astype(F32)
    for s in range(1, LAST):
        total = total + jnp.where(s < target, got[s].astype(F32), 0.0)
    return total


def state_kernel(z, got, z_out, copies):
    here = position()
    value = jnp.where(here == 0, z[...].astype(F32), summed(got, here)).astype(BF)
    z_out[...] = value
    for k in range(8):
        copies[k] = value


def final_kernel(target, got, out):
    out[0] = unpack(summed(got, jnp.concatenate([target[...], target[...]], axis=0)))


def call(body, out_shape, in_specs, scratch=(), limit=8):
    several = isinstance(out_shape, (list, tuple))
    return pl.pallas_call(
        body,
        out_shape=out_shape,
        in_specs=in_specs,
        out_specs=[VM] * len(out_shape) if several else VM,
        scratch_shapes=list(scratch),
        compiler_params=pltpu.CompilerParams(vmem_limit_bytes=limit * MIB),
    )


def shape(dims, dtype):
    return jax.ShapeDtypeStruct(dims, dtype)


def kept(dims, dtype):
    return pltpu.VMEM(dims, dtype)


def far(x):
    return pltpu.with_memory_space_constraint(x, pltpu.HBM)


def to_right(x, k):
    return lax.ppermute(x, "x", [(i, (i + k) % NX) for i in range(NX)])


def swap_cores(x):
    return lax.ppermute(x, "c", [(0, 1), (1, 0)])


def local(
    guesses, step_ids, step_sizes, slide, offsets, mod_table, w_in, w_qkv, qk_gain, w_out, w_fin
):
    state = guesses[0]
    z = pack(state.astype(BF))
    own = jnp.stack([z, swap_cores(z)])
    w_peer = swap_cores(lax.optimization_barrier((w_out, own))[0])
    zg = [own] + [to_right(own, NX - k) for k in range(1, NX)]
    operands = (offsets.T, qk_gain, w_in, mod_table.transpose(1, 0, 2), w_qkv)
    tab, wc, rows, w_in, w_qkv = call(
        prepare_kernel,
        [
            kept((4, 8, ROWS, HD), F32),
            kept((2 * C, D), BF),
            kept((8, D), F32),
            kept((C, D), BF),
            kept(w_qkv.shape, BF),
        ],
        [SM, VM] + [HB] * 5,
        PREPARE_SCRATCH,
        limit=12,
    )(step_ids, own, *[far(x) for x in operands])
    half = shape((S // 2, HL * HD), BF)
    row = shape((ROWS, D), BF)

    high = lax.ppermute(z, ("y", "z"), [(0, LAST)])

    mine, send = call(first_kernel, [half, half], [VM] * 8, BLOCK_SCRATCH, limit=16)(
        *zg, tab, wc, rows, w_qkv
    )
    operands = (w_out, w_fin.T, state)
    w_out, w_fin_rows, state = call(
        late_kernel,
        [kept(x.shape, x.dtype) for x in operands],
        [VM] + [HB] * 3,
        [pltpu.SemaphoreType.DMA((3,))],
    )(send, *[far(x) for x in operands])

    def gathered_drifts(mine, send, z, *extra):
        operands = (mine, swap_cores(send), w_out, w_peer)
        parts = call(out_kernel, [row] * NX, [VM] * 4, limit=16)(*operands)
        got = [parts[0]] + [to_right(parts[k], k) for k in (2, 1, 3)]
        outs, *extra = call(
            drift_kernel,
            [shape((NY * NZ, 16, 128), BF), *extra],
            [SM, SM] + [VM] * 10,
        )(step_sizes, slide, high, state, z, *got, w_in, rows, w_fin_rows)
        return lax.all_to_all(outs, ("y", "z"), 0, 0, tiled=True), *extra

    (got,) = gathered_drifts(mine, send, z)
    z, copies = call(
        state_kernel, [shape((16, 128), BF), shape((8, 16, 128), BF)], [VM] * 2
    )(z, got)
    zg = lax.all_to_all(copies, ("x", "c"), 0, 0, tiled=True)
    mine, send = call(second_kernel, [half, half], [VM] * 5, BLOCK_SCRATCH, limit=16)(
        zg, tab, wc, rows, w_qkv
    )
    got, target = gathered_drifts(mine, send, z, shape((8, 128), jnp.int32))
    return call(final_kernel, shape((1, ROWS, C), F32), [VM] * 2)(target, got)


def solution(mesh):
    grid = Mesh(mesh.devices.reshape(NY, NZ, NX, NC), ("y", "z", "x", "c"))
    step, head = ("y", "z"), ("x", "c")
    in_specs = (
        P(step, head, None),
        P(step),
        P(step),
        P(),
        P(),
        P(),
        P(),
        P(None, head),
        P(),
        P(head, None),
        P(),
    )
    out_specs = P(step, head, None)
    return jax.shard_map(local, mesh=grid, in_specs=in_specs, out_specs=out_specs, check_vma=False)
```

```python
import math

import jax
import jax.numpy as jnp
import numpy as np
from jax import lax
from jax.experimental import pallas as pl
from jax.experimental.pallas import tpu as pltpu
from jax.sharding import Mesh
from jax.sharding import PartitionSpec as P

NY, NZ, NX, NC = 4, 8, 4, 2
D = 3072
HD = 128
HL = 3
C = 64
S = 256
ROWS = 32
GRID_W = 16
ROT_DIM = 56
EPS = 1e-06
BF = jnp.bfloat16
F32 = jnp.float32
MIB = 1024 * 1024

VM = pl.BlockSpec(memory_space=pltpu.VMEM)
HB = pl.BlockSpec(memory_space=pltpu.HBM)
SM = pl.BlockSpec(memory_space=pltpu.SMEM)


def pack(x):
    return jnp.concatenate([x[:16], x[16:]], axis=1)


def unpack(x):
    return jnp.concatenate([x[:, :C], x[:, C:]], axis=0)


FREQ = [float(np.float32(10000.0 ** (-j * 2.0 / ROT_DIM))) for j in range(ROT_DIM // 2)]
QKV = 3 * HD


def swap_lanes(x):
    lane = lax.broadcasted_iota(jnp.int32, x.shape, len(x.shape) - 1)
    axis = len(x.shape) - 1
    return jnp.where(lane % 2 == 0, pltpu.roll(x, HD - 1, axis), pltpu.roll(x, 1, axis))


def halves(x):
    high = x.astype(BF)
    return high, (x - high.astype(F32)).astype(BF)


def prepare_kernel(
    step, after, offsets, gain, w_in, mod_table, w_qkv,
    tab, wc, rows, w_in_out, w_qkv_out,
    offv, gainv, modv, sems,
):
    at = jnp.clip(step[0], 0, mod_table.shape[1] - 1)
    block = pl.ds(pl.multiple_of(at // 8 * 8, 8), 8)
    pairs = [
        (offsets, offv),
        (gain, gainv),
        (w_in, w_in_out),
        (mod_table.at[:, block, :], modv),
        (w_qkv, w_qkv_out),
    ]
    copies = [pltpu.make_async_copy(a, b, sems.at[i]) for i, (a, b) in enumerate(pairs)]
    for copy in copies:
        copy.start()
    lane = lax.broadcasted_iota(jnp.int32, (1, HD), 1)
    pair = lane // 2
    by_row = jnp.zeros((1, HD), F32)
    by_col = jnp.zeros((1, HD), F32)
    count = ROT_DIM // 2
    for j in range(count):
        by_row = jnp.where(pair == HD // 2 - 2 * count + j, FREQ[j], by_row)
        by_col = jnp.where(pair == HD // 2 - count + j, FREQ[j], by_col)
    copies[0].wait()
    index = lax.broadcasted_iota(jnp.int32, (1, S), 1)
    row = (index // GRID_W + offv[0:1, :]).astype(F32)
    col = (index % GRID_W + offv[1:2, :]).astype(F32)
    both = jnp.concatenate([row, col, jnp.zeros((6, S), F32)], axis=0).T
    angle = both[:, 0:1] * by_row + both[:, 1:2] * by_col
    cosine = jnp.cos(angle)
    sine = jnp.sin(angle) * jnp.where(lane % 2 == 0, -1.0, 1.0)
    copies[1].wait()
    for k in range(2):
        g = gainv[k : k + 1, :]
        turned = swap_lanes(jnp.broadcast_to(g, (8, HD)))[0:1]
        tab[2 * k] = (cosine * g).reshape(8, ROWS, HD)
        tab[2 * k + 1] = (sine * turned).reshape(8, ROWS, HD)
    copies[2].wait()
    w = w_in_out[...].astype(F32)
    w = w - jnp.sum(w, axis=-1, keepdims=True) * (1.0 / D)
    high, low = halves(w)
    wc[:C, :] = high
    wc[C:, :] = low
    copies[3].wait()
    chosen = lax.broadcasted_iota(jnp.int32, (8, D), 0) == at % 8

    def pick(k):
        return jnp.sum(jnp.where(chosen, modv[k], 0.0), axis=0, keepdims=True)

    rows[0:1, :] = 1.0 + pick(1)
    rows[1:2, :] = pick(0)
    rows[2:3, :] = pick(2)
    rows[3:, :] = jnp.zeros((5, D), F32)
    for copy in copies[4:]:
        copy.wait()


PREPARE_SCRATCH = [
    pltpu.VMEM((2, S), jnp.int32),
    pltpu.VMEM((2, HD), F32),
    pltpu.VMEM((3, 8, D), F32),
    pltpu.SemaphoreType.DMA((5,)),
]


def block_body(chunk_of, tab, wc, rows, w_qkv, mine, send, zs, es, fs, qkv, qs):
    my_x, my_c = lax.axis_index("x"), lax.axis_index("c")
    order = [((my_x + r % 4) % 4) * 2 + (my_c + r // 4) % 2 for r in range(8)]
    for r in range(8):
        piece = chunk_of(r, order[r])
        zs[32 * r : 32 * r + 16, :] = piece[:, :C]
        zs[32 * r + 16 : 32 * r + 32, :] = piece[:, C:]
    z = zs[...]
    twice = jnp.concatenate([z, z], axis=1)
    total = jnp.zeros((S, 128), F32)
    for j in range(6):
        cut = slice(j * 512, j * 512 + 512)
        e = jnp.dot(twice, wc[:, cut], preferred_element_type=F32)
        es[:, cut] = e
        e = e * e
        total += (e[:, :128] + e[:, 128:256]) + (e[:, 256:384] + e[:, 384:])
    scale = lax.rsqrt(jnp.sum(total, axis=-1, keepdims=True) * (1.0 / D) + EPS)
    for j in range(6):
        cut = slice(j * 512, j * 512 + 512)
        fs[:, cut] = (es[:, cut] * scale * rows[0:1, cut] + rows[1:2, cut]).astype(BF)
    qkv[...] = jnp.dot(fs[...], w_qkv[...], preferred_element_type=F32)
    mean = jnp.full((2 * HD, HD), 1.0 / HD, BF)

    def table(k):
        return jnp.concatenate([tab[k, order[r]] for r in range(8)], axis=0)

    def turned(x, k):
        high, low = halves(x * x)
        square = jnp.dot(jnp.concatenate([high, low], axis=1), mean, preferred_element_type=F32)
        x = x * table(2 * k) + swap_lanes(x) * table(2 * k + 1)
        return (x * lax.rsqrt(square + EPS)).astype(BF)

    for head in range(HL):
        base = head * QKV
        for k in range(2):
            qs[head, k] = turned(qkv[:, base + k * HD : base + k * HD + HD], k)
        qs[head, 2] = qkv[:, base + 2 * HD : base + QKV].astype(BF)
    scores = [
        lax.dot_general(
            qs[head, 0], qs[head, 1], (((1,), (1,)), ((), ())), preferred_element_type=F32
        )
        for head in range(HL)
    ]
    tops = [jnp.max(score, axis=-1, keepdims=True) for score in scores]
    factor = math.log2(math.e) / math.sqrt(HD)
    probs = [jnp.exp2((score - top) * factor) for score, top in zip(scores, tops)]
    totals = [jnp.sum(p, axis=-1, keepdims=True) for p in probs]
    outs = [
        jnp.dot(p.astype(BF), qs[head, 2], preferred_element_type=F32)
        for head, p in enumerate(probs)
    ]
    for head in range(HL):
        out = (outs[head] * (1.0 / totals[head])).astype(BF)
        mine[:, head * HD : head * HD + HD] = out[: S // 2]
        send[:, head * HD : head * HD + HD] = out[S // 2 :]


def first_kernel(z0, z1, z2, z3, *rest):
    z = (z0, z1, z2, z3)
    block_body(lambda r, i: z[r % 4][r // 4], *rest)


def second_kernel(zg, *rest):
    block_body(lambda r, i: zg[i], *rest)


BLOCK_SCRATCH = [
    pltpu.VMEM((S, C), BF),
    pltpu.VMEM((S, D), F32),
    pltpu.VMEM((S, D), BF),
    pltpu.VMEM((S, HL * QKV), F32),
    pltpu.VMEM((HL, 3, S, HD), BF),
]


def projected(mine, peer, w_mine, w_peer, cut):
    middle = jnp.concatenate([mine[:, 2 * HD :], peer[:, :HD]], axis=1)
    w_middle = jnp.concatenate([w_mine[2 * HD :, cut], w_peer[:HD, cut]], axis=0)
    part = jnp.dot(mine[:, : 2 * HD], w_mine[: 2 * HD, cut], preferred_element_type=F32)
    part += jnp.dot(middle, w_middle, preferred_element_type=F32)
    part += jnp.dot(peer[:, HD:], w_peer[HD:, cut], preferred_element_type=F32)
    return part.astype(BF)


def out_kernel(mine, peer, w_mine, w_peer, *outs):
    for j in range(6):
        cut = slice(j * 512, j * 512 + 512)
        part = projected(mine, peer, w_mine, w_peer, cut)
        for k in range(NX):
            outs[k][:, cut] = part[ROWS * k : ROWS * (k + 1)]


def position():
    return lax.axis_index("y") * NZ + lax.axis_index("z")


LAST = NY * NZ - 1


def drift_kernel(
    size, slide, high, zstart, z, p0, p1, p2, p3, w_in, gate, w_fin, out, target=None
):
    e = jnp.dot(unpack(z[...]), w_in[...], preferred_element_type=F32)
    attn = p0[...].astype(F32) + p1[...].astype(F32) + p2[...].astype(F32) + p3[...].astype(F32)
    h = e + gate[2:3, :] * attn
    mean = jnp.sum(h, axis=-1, keepdims=True) * (1.0 / D)
    h = h - mean
    var = jnp.sum(h * h, axis=-1, keepdims=True) * (1.0 / D)
    normed = (h * lax.rsqrt(var + EPS)).astype(BF)
    drift = size[0] * lax.dot_general(
        normed, w_fin[...], (((1,), (1,)), ((), ())), preferred_element_type=F32
    )
    here = position()
    low = zstart[...] - zstart[...].astype(BF).astype(F32)
    value = pack(drift + jnp.where(here == 0, low, 0.0)).astype(BF)
    value = jnp.where(here == LAST, high[...].astype(F32), value.astype(F32)).astype(BF)
    for k in range(out.shape[0]):
        out[k] = value
    if target is not None:
        target[...] = jnp.full((8, 128), jnp.minimum(here + slide[0], LAST), jnp.int32)


def summed(got, target):
    total = got[0].astype(F32) + got[LAST].astype(F32)
    for s in range(1, LAST):
        total = total + jnp.where(s < target, got[s].astype(F32), 0.0)
    return total


def state_kernel(z, got, z_out, copies):
    here = position()
    value = jnp.where(here == 0, z[...].astype(F32), summed(got, here)).astype(BF)
    z_out[...] = value
    for k in range(8):
        copies[k] = value


def final_kernel(target, got, out):
    out[0] = unpack(summed(got, jnp.concatenate([target[...], target[...]], axis=0)))


def call(body, out_shape, in_specs, scratch=(), limit=8):
    several = isinstance(out_shape, (list, tuple))
    return pl.pallas_call(
        body,
        out_shape=out_shape,
        in_specs=in_specs,
        out_specs=[VM] * len(out_shape) if several else VM,
        scratch_shapes=list(scratch),
        compiler_params=pltpu.CompilerParams(vmem_limit_bytes=limit * MIB),
    )


def shape(dims, dtype):
    return jax.ShapeDtypeStruct(dims, dtype)


def kept(dims, dtype):
    return pltpu.VMEM(dims, dtype)


def far(x):
    return pltpu.with_memory_space_constraint(x, pltpu.HBM)


def to_right(x, k):
    return lax.ppermute(x, "x", [(i, (i + k) % NX) for i in range(NX)])


def swap_cores(x):
    return lax.ppermute(x, "c", [(0, 1), (1, 0)])


def local(
    guesses, step_ids, step_sizes, slide, offsets, mod_table, w_in, w_qkv, qk_gain, w_out, w_fin
):
    state = guesses[0]
    z = pack(state.astype(BF))
    own = jnp.stack([z, swap_cores(z)])
    w_peer = swap_cores(lax.optimization_barrier((w_out, own))[0])
    zg = [own] + [to_right(own, NX - k) for k in range(1, NX)]
    operands = (offsets.T, qk_gain, w_in, mod_table.transpose(1, 0, 2), w_qkv)
    tab, wc, rows, w_in, w_qkv = call(
        prepare_kernel,
        [
            kept((4, 8, ROWS, HD), F32),
            kept((2 * C, D), BF),
            kept((8, D), F32),
            kept((C, D), BF),
            kept(w_qkv.shape, BF),
        ],
        [SM, VM] + [HB] * 5,
        PREPARE_SCRATCH,
        limit=12,
    )(step_ids, own, *[far(x) for x in operands])
    half = shape((S // 2, HL * HD), BF)
    row = shape((ROWS, D), BF)

    high = lax.ppermute(z, ("y", "z"), [(0, LAST)])

    mine, send = call(first_kernel, [half, half], [VM] * 8, BLOCK_SCRATCH, limit=16)(
        *zg, tab, wc, rows, w_qkv
    )
    w_fin_rows = w_fin.T

    def gathered_drifts(mine, send, z, *extra):
        operands = (mine, swap_cores(send), w_out, w_peer)
        parts = call(out_kernel, [row] * NX, [VM] * 4, limit=16)(*operands)
        got = [parts[0]] + [to_right(parts[k], k) for k in (2, 1, 3)]
        outs, *extra = call(
            drift_kernel,
            [shape((NY * NZ, 16, 128), BF), *extra],
            [SM, SM] + [VM] * 10,
        )(step_sizes, slide, high, state, z, *got, w_in, rows, w_fin_rows)
        got = lax.all_to_all(outs, ("y", "z"), 0, 0, tiled=True)
        return got, *extra

    (got,) = gathered_drifts(mine, send, z)
    z, copies = call(
        state_kernel, [shape((16, 128), BF), shape((8, 16, 128), BF)], [VM] * 2
    )(z, got)
    zg = lax.all_to_all(copies, ("x", "c"), 0, 0, tiled=True)
    mine, send = call(second_kernel, [half, half], [VM] * 5, BLOCK_SCRATCH, limit=16)(
        zg, tab, wc, rows, w_qkv
    )
    got, target = gathered_drifts(mine, send, z, shape((8, 128), jnp.int32))
    return call(final_kernel, shape((1, ROWS, C), F32), [VM] * 2)(target, got)


def solution(mesh):
    grid = Mesh(mesh.devices.reshape(NY, NZ, NX, NC), ("y", "z", "x", "c"))
    step, head = ("y", "z"), ("x", "c")
    in_specs = (
        P(step, head, None),
        P(step),
        P(step),
        P(),
        P(),
        P(),
        P(),
        P(None, head),
        P(),
        P(head, None),
        P(),
    )
    out_specs = P(step, head, None)
    return jax.shard_map(local, mesh=grid, in_specs=in_specs, out_specs=out_specs, check_vma=False)
```

```python
import math

import jax
import jax.numpy as jnp
import numpy as np
from jax import lax
from jax.experimental import pallas as pl
from jax.experimental.pallas import tpu as pltpu
from jax.sharding import Mesh
from jax.sharding import PartitionSpec as P

NY, NZ, NX, NC = 4, 8, 4, 2
D = 3072
HD = 128
HL = 3
C = 64
S = 256
ROWS = 32
GRID_W = 16
ROT_DIM = 56
EPS = 1e-06
BF = jnp.bfloat16
F32 = jnp.float32
MIB = 1024 * 1024

VM = pl.BlockSpec(memory_space=pltpu.VMEM)
HB = pl.BlockSpec(memory_space=pltpu.HBM)
SM = pl.BlockSpec(memory_space=pltpu.SMEM)


def pack(x):
    return jnp.concatenate([x[:16], x[16:]], axis=1)


def unpack(x):
    return jnp.concatenate([x[:, :C], x[:, C:]], axis=0)


FREQ = [float(np.float32(10000.0 ** (-j * 2.0 / ROT_DIM))) for j in range(ROT_DIM // 2)]
QKV = 3 * HD


def swap_lanes(x):
    lane = lax.broadcasted_iota(jnp.int32, x.shape, len(x.shape) - 1)
    axis = len(x.shape) - 1
    return jnp.where(lane % 2 == 0, pltpu.roll(x, HD - 1, axis), pltpu.roll(x, 1, axis))


def halves(x):
    high = x.astype(BF)
    return high, (x - high.astype(F32)).astype(BF)


def prepare_kernel(
    step, after, offsets, gain, w_in, mod_table, w_qkv,
    tab, wc, rows, w_in_out, w_qkv_out,
    offv, gainv, modv, sems,
):
    at = jnp.clip(step[0], 0, mod_table.shape[1] - 1)
    block = pl.ds(pl.multiple_of(at // 8 * 8, 8), 8)
    pairs = [
        (offsets, offv),
        (gain, gainv),
        (w_in, w_in_out),
        (mod_table.at[:, block, :], modv),
        (w_qkv, w_qkv_out),
    ]
    copies = [pltpu.make_async_copy(a, b, sems.at[i]) for i, (a, b) in enumerate(pairs)]
    for copy in copies:
        copy.start()
    lane = lax.broadcasted_iota(jnp.int32, (1, HD), 1)
    pair = lane // 2
    by_row = jnp.zeros((1, HD), F32)
    by_col = jnp.zeros((1, HD), F32)
    count = ROT_DIM // 2
    for j in range(count):
        by_row = jnp.where(pair == HD // 2 - 2 * count + j, FREQ[j], by_row)
        by_col = jnp.where(pair == HD // 2 - count + j, FREQ[j], by_col)
    copies[0].wait()
    index = lax.broadcasted_iota(jnp.int32, (1, S), 1)
    row = (index // GRID_W + offv[0:1, :]).astype(F32)
    col = (index % GRID_W + offv[1:2, :]).astype(F32)
    both = jnp.concatenate([row, col, jnp.zeros((6, S), F32)], axis=0).T
    angle = both[:, 0:1] * by_row + both[:, 1:2] * by_col
    cosine = jnp.cos(angle)
    sine = jnp.sin(angle) * jnp.where(lane % 2 == 0, -1.0, 1.0)
    copies[1].wait()
    for k in range(2):
        g = gainv[k : k + 1, :]
        turned = swap_lanes(jnp.broadcast_to(g, (8, HD)))[0:1]
        tab[2 * k] = (cosine * g).reshape(8, ROWS, HD)
        tab[2 * k + 1] = (sine * turned).reshape(8, ROWS, HD)
    copies[2].wait()
    w = w_in_out[...].astype(F32)
    w = w - jnp.sum(w, axis=-1, keepdims=True) * (1.0 / D)
    high, low = halves(w)
    wc[:C, :] = high
    wc[C:, :] = low
    copies[3].wait()
    chosen = lax.broadcasted_iota(jnp.int32, (8, D), 0) == at % 8

    def pick(k):
        return jnp.sum(jnp.where(chosen, modv[k], 0.0), axis=0, keepdims=True)

    rows[0:1, :] = 1.0 + pick(1)
    rows[1:2, :] = pick(0)
    rows[2:3, :] = pick(2)
    rows[3:, :] = jnp.zeros((5, D), F32)
    for copy in copies[4:]:
        copy.wait()


PREPARE_SCRATCH = [
    pltpu.VMEM((2, S), jnp.int32),
    pltpu.VMEM((2, HD), F32),
    pltpu.VMEM((3, 8, D), F32),
    pltpu.SemaphoreType.DMA((5,)),
]


def block_body(chunk_of, tab, wc, rows, w_qkv, mine, send, zs, es, fs, qkv, qs):
    my_x, my_c = lax.axis_index("x"), lax.axis_index("c")
    order = [((my_x + r % 4) % 4) * 2 + (my_c + r // 4) % 2 for r in range(8)]
    for r in range(8):
        piece = chunk_of(r, order[r])
        zs[32 * r : 32 * r + 16, :] = piece[:, :C]
        zs[32 * r + 16 : 32 * r + 32, :] = piece[:, C:]
    z = zs[...]
    twice = jnp.concatenate([z, z], axis=1)
    total = jnp.zeros((S, 128), F32)
    for j in range(6):
        cut = slice(j * 512, j * 512 + 512)
        e = jnp.dot(twice, wc[:, cut], preferred_element_type=F32)
        es[:, cut] = e
        e = e * e
        total += (e[:, :128] + e[:, 128:256]) + (e[:, 256:384] + e[:, 384:])
    scale = lax.rsqrt(jnp.sum(total, axis=-1, keepdims=True) * (1.0 / D) + EPS)
    for j in range(6):
        cut = slice(j * 512, j * 512 + 512)
        fs[:, cut] = (es[:, cut] * scale * rows[0:1, cut] + rows[1:2, cut]).astype(BF)
    qkv[...] = jnp.dot(fs[...], w_qkv[...], preferred_element_type=F32)
    mean = jnp.full((2 * HD, HD), 1.0 / HD, BF)

    def table(k):
        return jnp.concatenate([tab[k, order[r]] for r in range(8)], axis=0)

    def turned(x, k):
        high, low = halves(x * x)
        square = jnp.dot(jnp.concatenate([high, low], axis=1), mean, preferred_element_type=F32)
        x = x * table(2 * k) + swap_lanes(x) * table(2 * k + 1)
        return (x * lax.rsqrt(square + EPS)).astype(BF)

    for head in range(HL):
        base = head * QKV
        for k in range(2):
            qs[head, k] = turned(qkv[:, base + k * HD : base + k * HD + HD], k)
        qs[head, 2] = qkv[:, base + 2 * HD : base + QKV].astype(BF)
    scores = [
        lax.dot_general(
            qs[head, 0], qs[head, 1], (((1,), (1,)), ((), ())), preferred_element_type=F32
        )
        for head in range(HL)
    ]
    tops = [jnp.max(score, axis=-1, keepdims=True) for score in scores]
    factor = math.log2(math.e) / math.sqrt(HD)
    probs = [jnp.exp2((score - top) * factor) for score, top in zip(scores, tops)]
    totals = [jnp.sum(p, axis=-1, keepdims=True) for p in probs]
    outs = [
        jnp.dot(p.astype(BF), qs[head, 2], preferred_element_type=F32)
        for head, p in enumerate(probs)
    ]
    for head in range(HL):
        out = (outs[head] * (1.0 / totals[head])).astype(BF)
        mine[:, head * HD : head * HD + HD] = out[: S // 2]
        send[:, head * HD : head * HD + HD] = out[S // 2 :]


def first_kernel(z0, z1, z2, z3, *rest):
    z = (z0, z1, z2, z3)
    block_body(lambda r, i: z[r % 4][r // 4], *rest)


def second_kernel(zg, *rest):
    block_body(lambda r, i: zg[i], *rest)


BLOCK_SCRATCH = [
    pltpu.VMEM((S, C), BF),
    pltpu.VMEM((S, D), F32),
    pltpu.VMEM((S, D), BF),
    pltpu.VMEM((S, HL * QKV), F32),
    pltpu.VMEM((HL, 3, S, HD), BF),
]


def own_kernel(after, mine, w_mine, z, w_in, out, embed):
    embed[...] = jnp.dot(unpack(z[...]), w_in[...], preferred_element_type=F32)
    for j in range(6):
        cut = slice(j * 512, j * 512 + 512)
        out[:, cut] = jnp.dot(mine[...], w_mine[:, cut], preferred_element_type=F32)


def sum_kernel(part, peer, w_peer, *outs):
    for j in range(6):
        cut = slice(j * 512, j * 512 + 512)
        total = part[:, cut] + jnp.dot(peer[...], w_peer[:, cut], preferred_element_type=F32)
        total = total.astype(BF)
        for k in range(NX):
            outs[k][:, cut] = total[ROWS * k : ROWS * (k + 1)]


def position():
    return lax.axis_index("y") * NZ + lax.axis_index("z")


LAST = NY * NZ - 1


def drift_kernel(
    size, slide, high, zstart, embed, p0, p1, p2, p3, gate, w_fin, out, target=None
):
    attn = p0[...].astype(F32) + p1[...].astype(F32) + p2[...].astype(F32) + p3[...].astype(F32)
    h = embed[...] + gate[2:3, :] * attn
    mean = jnp.sum(h, axis=-1, keepdims=True) * (1.0 / D)
    h = h - mean
    var = jnp.sum(h * h, axis=-1, keepdims=True) * (1.0 / D)
    normed = (h * lax.rsqrt(var + EPS)).astype(BF)
    drift = size[0] * lax.dot_general(
        normed, w_fin[...], (((1,), (1,)), ((), ())), preferred_element_type=F32
    )
    here = position()
    low = zstart[...] - zstart[...].astype(BF).astype(F32)
    value = pack(drift + jnp.where(here == 0, low, 0.0)).astype(BF)
    value = jnp.where(here == LAST, high[...].astype(F32), value.astype(F32)).astype(BF)
    for k in range(out.shape[0]):
        out[k] = value
    if target is not None:
        target[...] = jnp.full((8, 128), jnp.minimum(here + slide[0], LAST), jnp.int32)


def summed(got, target):
    total = got[0].astype(F32) + got[LAST].astype(F32)
    for s in range(1, LAST):
        total = total + jnp.where(s < target, got[s].astype(F32), 0.0)
    return total


def state_kernel(z, got, z_out, copies):
    here = position()
    value = jnp.where(here == 0, z[...].astype(F32), summed(got, here)).astype(BF)
    z_out[...] = value
    for k in range(8):
        copies[k] = value


def final_kernel(target, got, out):
    out[0] = unpack(summed(got, jnp.concatenate([target[...], target[...]], axis=0)))


def call(body, out_shape, in_specs, scratch=(), limit=8):
    several = isinstance(out_shape, (list, tuple))
    return pl.pallas_call(
        body,
        out_shape=out_shape,
        in_specs=in_specs,
        out_specs=[VM] * len(out_shape) if several else VM,
        scratch_shapes=list(scratch),
        compiler_params=pltpu.CompilerParams(vmem_limit_bytes=limit * MIB),
    )


def shape(dims, dtype):
    return jax.ShapeDtypeStruct(dims, dtype)


def kept(dims, dtype):
    return pltpu.VMEM(dims, dtype)


def far(x):
    return pltpu.with_memory_space_constraint(x, pltpu.HBM)


def to_right(x, k):
    return lax.ppermute(x, "x", [(i, (i + k) % NX) for i in range(NX)])


def swap_cores(x):
    return lax.ppermute(x, "c", [(0, 1), (1, 0)])


def local(
    guesses, step_ids, step_sizes, slide, offsets, mod_table, w_in, w_qkv, qk_gain, w_out, w_fin
):
    state = guesses[0]
    z = pack(state.astype(BF))
    own = jnp.stack([z, swap_cores(z)])
    w_peer = swap_cores(lax.optimization_barrier((w_out, own))[0])
    zg = [own] + [to_right(own, NX - k) for k in range(1, NX)]
    operands = (offsets.T, qk_gain, w_in, mod_table.transpose(1, 0, 2), w_qkv)
    tab, wc, rows, w_in, w_qkv = call(
        prepare_kernel,
        [
            kept((4, 8, ROWS, HD), F32),
            kept((2 * C, D), BF),
            kept((8, D), F32),
            kept((C, D), BF),
            kept(w_qkv.shape, BF),
        ],
        [SM, VM] + [HB] * 5,
        PREPARE_SCRATCH,
        limit=12,
    )(step_ids, own, *[far(x) for x in operands])
    half = shape((S // 2, HL * HD), BF)
    row = shape((ROWS, D), BF)

    high = lax.ppermute(z, ("y", "z"), [(0, LAST)])

    mine, send = call(first_kernel, [half, half], [VM] * 8, BLOCK_SCRATCH, limit=16)(
        *zg, tab, wc, rows, w_qkv
    )
    w_fin_rows = w_fin.T

    def gathered_drifts(mine, send, z, *extra):
        peer = swap_cores(send)
        part, embed = call(
            own_kernel, [shape((S // 2, D), F32), shape((ROWS, D), F32)], [VM] * 5, limit=16
        )(send, mine, w_out, z, w_in)
        parts = call(sum_kernel, [row] * NX, [VM] * 3, limit=16)(part, peer, w_peer)
        got = [parts[0]] + [to_right(parts[k], k) for k in (2, 1, 3)]
        outs, *extra = call(
            drift_kernel,
            [shape((NY * NZ, 16, 128), BF), *extra],
            [SM, SM] + [VM] * 9,
        )(step_sizes, slide, high, state, embed, *got, rows, w_fin_rows)
        got = lax.all_to_all(outs, ("y", "z"), 0, 0, tiled=True)
        return got, *extra

    (got,) = gathered_drifts(mine, send, z)
    z, copies = call(
        state_kernel, [shape((16, 128), BF), shape((8, 16, 128), BF)], [VM] * 2
    )(z, got)
    zg = lax.all_to_all(copies, ("x", "c"), 0, 0, tiled=True)
    mine, send = call(second_kernel, [half, half], [VM] * 5, BLOCK_SCRATCH, limit=16)(
        zg, tab, wc, rows, w_qkv
    )
    got, target = gathered_drifts(mine, send, z, shape((8, 128), jnp.int32))
    return call(final_kernel, shape((1, ROWS, C), F32), [VM] * 2)(target, got)


def solution(mesh):
    grid = Mesh(mesh.devices.reshape(NY, NZ, NX, NC), ("y", "z", "x", "c"))
    step, head = ("y", "z"), ("x", "c")
    in_specs = (
        P(step, head, None),
        P(step),
        P(step),
        P(),
        P(),
        P(),
        P(),
        P(None, head),
        P(),
        P(head, None),
        P(),
    )
    out_specs = P(step, head, None)
    return jax.shard_map(local, mesh=grid, in_specs=in_specs, out_specs=out_specs, check_vma=False)
```

```python
import math

import jax
import jax.numpy as jnp
import numpy as np
from jax import lax
from jax.experimental import pallas as pl
from jax.experimental.pallas import tpu as pltpu
from jax.sharding import Mesh
from jax.sharding import PartitionSpec as P

NY, NZ, NX, NC = 4, 8, 4, 2
D = 3072
HD = 128
HL = 3
C = 64
S = 256
ROWS = 32
GRID_W = 16
ROT_DIM = 56
EPS = 1e-06
BF = jnp.bfloat16
F32 = jnp.float32
MIB = 1024 * 1024

VM = pl.BlockSpec(memory_space=pltpu.VMEM)
HB = pl.BlockSpec(memory_space=pltpu.HBM)
SM = pl.BlockSpec(memory_space=pltpu.SMEM)


def pack(x):
    return jnp.concatenate([x[:16], x[16:]], axis=1)


def unpack(x):
    return jnp.concatenate([x[:, :C], x[:, C:]], axis=0)


FREQ = [float(np.float32(10000.0 ** (-j * 2.0 / ROT_DIM))) for j in range(ROT_DIM // 2)]
QKV = 3 * HD


def swap_lanes(x):
    lane = lax.broadcasted_iota(jnp.int32, x.shape, len(x.shape) - 1)
    axis = len(x.shape) - 1
    return jnp.where(lane % 2 == 0, pltpu.roll(x, HD - 1, axis), pltpu.roll(x, 1, axis))


def halves(x):
    high = x.astype(BF)
    return high, (x - high.astype(F32)).astype(BF)


def stack_kernel(z, other, own):
    own[0] = z[...]
    own[1] = pack(other[0].astype(BF))


def prepare_kernel(
    step, after, offsets, gain, w_in, mod_table, w_qkv,
    tab, wc, rows, w_in_out, w_qkv_out,
    offv, gainv, modv, sems,
):
    at = jnp.clip(step[0], 0, mod_table.shape[1] - 1)
    block = pl.ds(pl.multiple_of(at // 8 * 8, 8), 8)
    pairs = [
        (offsets, offv),
        (gain, gainv),
        (w_in, w_in_out),
        (mod_table.at[:, block, :], modv),
        (w_qkv, w_qkv_out),
    ]
    copies = [pltpu.make_async_copy(a, b, sems.at[i]) for i, (a, b) in enumerate(pairs)]
    for copy in copies:
        copy.start()
    lane = lax.broadcasted_iota(jnp.int32, (1, HD), 1)
    pair = lane // 2
    by_row = jnp.zeros((1, HD), F32)
    by_col = jnp.zeros((1, HD), F32)
    count = ROT_DIM // 2
    for j in range(count):
        by_row = jnp.where(pair == HD // 2 - 2 * count + j, FREQ[j], by_row)
        by_col = jnp.where(pair == HD // 2 - count + j, FREQ[j], by_col)
    copies[0].wait()
    index = lax.broadcasted_iota(jnp.int32, (1, S), 1)
    row = (index // GRID_W + offv[0:1, :]).astype(F32)
    col = (index % GRID_W + offv[1:2, :]).astype(F32)
    both = jnp.concatenate([row, col, jnp.zeros((6, S), F32)], axis=0).T
    angle = both[:, 0:1] * by_row + both[:, 1:2] * by_col
    cosine = jnp.cos(angle)
    sine = jnp.sin(angle) * jnp.where(lane % 2 == 0, -1.0, 1.0)
    copies[1].wait()
    for k in range(2):
        g = gainv[k : k + 1, :]
        turned = swap_lanes(jnp.broadcast_to(g, (8, HD)))[0:1]
        tab[2 * k] = (cosine * g).reshape(8, ROWS, HD)
        tab[2 * k + 1] = (sine * turned).reshape(8, ROWS, HD)
    copies[2].wait()
    w = w_in_out[...].astype(F32)
    w = w - jnp.sum(w, axis=-1, keepdims=True) * (1.0 / D)
    high, low = halves(w)
    wc[:C, :] = high
    wc[C:, :] = low
    copies[3].wait()
    chosen = lax.broadcasted_iota(jnp.int32, (8, D), 0) == at % 8

    def pick(k):
        return jnp.sum(jnp.where(chosen, modv[k], 0.0), axis=0, keepdims=True)

    rows[0:1, :] = 1.0 + pick(1)
    rows[1:2, :] = pick(0)
    rows[2:3, :] = pick(2)
    rows[3:, :] = jnp.zeros((5, D), F32)
    for copy in copies[4:]:
        copy.wait()


PREPARE_SCRATCH = [
    pltpu.VMEM((2, S), jnp.int32),
    pltpu.VMEM((2, HD), F32),
    pltpu.VMEM((3, 8, D), F32),
    pltpu.SemaphoreType.DMA((5,)),
]


def block_body(chunk_of, tab, wc, rows, w_qkv, mine, send, zs, es, fs, qkv, qs):
    my_x, my_c = lax.axis_index("x"), lax.axis_index("c")
    order = [((my_x + r % 4) % 4) * 2 + (my_c + r // 4) % 2 for r in range(8)]
    for r in range(8):
        piece = chunk_of(r, order[r])
        zs[32 * r : 32 * r + 16, :] = piece[:, :C]
        zs[32 * r + 16 : 32 * r + 32, :] = piece[:, C:]
    z = zs[...]
    twice = jnp.concatenate([z, z], axis=1)
    total = jnp.zeros((S, 128), F32)
    for j in range(6):
        cut = slice(j * 512, j * 512 + 512)
        e = jnp.dot(twice, wc[:, cut], preferred_element_type=F32)
        es[:, cut] = e
        e = e * e
        total += (e[:, :128] + e[:, 128:256]) + (e[:, 256:384] + e[:, 384:])
    scale = lax.rsqrt(jnp.sum(total, axis=-1, keepdims=True) * (1.0 / D) + EPS)
    for j in range(6):
        cut = slice(j * 512, j * 512 + 512)
        fs[:, cut] = (es[:, cut] * scale * rows[0:1, cut] + rows[1:2, cut]).astype(BF)
    qkv[...] = jnp.dot(fs[...], w_qkv[...], preferred_element_type=F32)
    mean = jnp.full((2 * HD, HD), 1.0 / HD, BF)

    def table(k):
        return jnp.concatenate([tab[k, order[r]] for r in range(8)], axis=0)

    def turned(x, k):
        high, low = halves(x * x)
        square = jnp.dot(jnp.concatenate([high, low], axis=1), mean, preferred_element_type=F32)
        x = x * table(2 * k) + swap_lanes(x) * table(2 * k + 1)
        return (x * lax.rsqrt(square + EPS)).astype(BF)

    for head in range(HL):
        base = head * QKV
        for k in range(2):
            qs[head, k] = turned(qkv[:, base + k * HD : base + k * HD + HD], k)
        qs[head, 2] = qkv[:, base + 2 * HD : base + QKV].astype(BF)
    scores = [
        lax.dot_general(
            qs[head, 0], qs[head, 1], (((1,), (1,)), ((), ())), preferred_element_type=F32
        )
        for head in range(HL)
    ]
    tops = [jnp.max(score, axis=-1, keepdims=True) for score in scores]
    factor = math.log2(math.e) / math.sqrt(HD)
    probs = [jnp.exp2((score - top) * factor) for score, top in zip(scores, tops)]
    totals = [jnp.sum(p, axis=-1, keepdims=True) for p in probs]
    outs = [
        jnp.dot(p.astype(BF), qs[head, 2], preferred_element_type=F32)
        for head, p in enumerate(probs)
    ]
    for head in range(HL):
        out = (outs[head] * (1.0 / totals[head])).astype(BF)
        mine[:, head * HD : head * HD + HD] = out[: S // 2]
        send[:, head * HD : head * HD + HD] = out[S // 2 :]


def first_kernel(z0, z1, z2, z3, *rest):
    z = (z0, z1, z2, z3)
    block_body(lambda r, i: z[r % 4][r // 4], *rest)


def second_kernel(zg, *rest):
    block_body(lambda r, i: zg[i], *rest)


BLOCK_SCRATCH = [
    pltpu.VMEM((S, C), BF),
    pltpu.VMEM((S, D), F32),
    pltpu.VMEM((S, D), BF),
    pltpu.VMEM((S, HL * QKV), F32),
    pltpu.VMEM((HL, 3, S, HD), BF),
]


def own_kernel(after, mine, w_mine, z, w_in, out, embed):
    embed[...] = jnp.dot(unpack(z[...]), w_in[...], preferred_element_type=F32)
    for j in range(6):
        cut = slice(j * 512, j * 512 + 512)
        out[:, cut] = jnp.dot(mine[...], w_mine[:, cut], preferred_element_type=F32)


def sum_kernel(part, peer, w_peer, *outs):
    for j in range(6):
        cut = slice(j * 512, j * 512 + 512)
        total = part[:, cut] + jnp.dot(peer[...], w_peer[:, cut], preferred_element_type=F32)
        total = total.astype(BF)
        for k in range(NX):
            outs[k][:, cut] = total[ROWS * k : ROWS * (k + 1)]


def position():
    return lax.axis_index("y") * NZ + lax.axis_index("z")


LAST = NY * NZ - 1


def drift_kernel(
    size, slide, high, zstart, embed, p0, p1, p2, p3, gate, w_fin, out, target=None
):
    attn = p0[...].astype(F32) + p1[...].astype(F32) + p2[...].astype(F32) + p3[...].astype(F32)
    h = embed[...] + gate[2:3, :] * attn
    mean = jnp.sum(h, axis=-1, keepdims=True) * (1.0 / D)
    h = h - mean
    var = jnp.sum(h * h, axis=-1, keepdims=True) * (1.0 / D)
    normed = (h * lax.rsqrt(var + EPS)).astype(BF)
    drift = size[0] * lax.dot_general(
        normed, w_fin[...], (((1,), (1,)), ((), ())), preferred_element_type=F32
    )
    here = position()
    low = zstart[...] - zstart[...].astype(BF).astype(F32)
    value = pack(drift + jnp.where(here == 0, low, 0.0)).astype(BF)
    value = jnp.where(here == LAST, high[...].astype(F32), value.astype(F32)).astype(BF)
    for k in range(out.shape[0]):
        out[k] = value
    if target is not None:
        target[...] = jnp.full((8, 128), jnp.minimum(here + slide[0], LAST), jnp.int32)


def summed(got, target):
    total = got[0].astype(F32) + got[LAST].astype(F32)
    for s in range(1, LAST):
        total = total + jnp.where(s < target, got[s].astype(F32), 0.0)
    return total


def state_kernel(z, got, z_out, copies):
    here = position()
    value = jnp.where(here == 0, z[...].astype(F32), summed(got, here)).astype(BF)
    z_out[...] = value
    for k in range(8):
        copies[k] = value


def final_kernel(target, got, out):
    out[0] = unpack(summed(got, jnp.concatenate([target[...], target[...]], axis=0)))


def call(body, out_shape, in_specs, scratch=(), limit=8):
    several = isinstance(out_shape, (list, tuple))
    return pl.pallas_call(
        body,
        out_shape=out_shape,
        in_specs=in_specs,
        out_specs=[VM] * len(out_shape) if several else VM,
        scratch_shapes=list(scratch),
        compiler_params=pltpu.CompilerParams(vmem_limit_bytes=limit * MIB),
    )


def shape(dims, dtype):
    return jax.ShapeDtypeStruct(dims, dtype)


def kept(dims, dtype):
    return pltpu.VMEM(dims, dtype)


def far(x):
    return pltpu.with_memory_space_constraint(x, pltpu.HBM)


def to_right(x, k):
    return lax.ppermute(x, "x", [(i, (i + k) % NX) for i in range(NX)])


def swap_cores(x):
    return lax.ppermute(x, "c", [(0, 1), (1, 0)])


def local(
    guesses, step_ids, step_sizes, slide, offsets, mod_table, w_in, w_qkv, qk_gain, w_out, w_fin
):
    state = guesses[0]
    z = pack(state.astype(BF))
    own = call(stack_kernel, shape((2, 16, 128), BF), [VM] * 2)(z, swap_cores(guesses))
    w_peer = swap_cores(lax.optimization_barrier((w_out, own))[0])
    zg = [own] + [to_right(own, NX - k) for k in range(1, NX)]
    operands = (offsets.T, qk_gain, w_in, mod_table.transpose(1, 0, 2), w_qkv)
    tab, wc, rows, w_in, w_qkv = call(
        prepare_kernel,
        [
            kept((4, 8, ROWS, HD), F32),
            kept((2 * C, D), BF),
            kept((8, D), F32),
            kept((C, D), BF),
            kept(w_qkv.shape, BF),
        ],
        [SM, VM] + [HB] * 5,
        PREPARE_SCRATCH,
        limit=12,
    )(step_ids, own, *[far(x) for x in operands])
    half = shape((S // 2, HL * HD), BF)
    row = shape((ROWS, D), BF)

    high = lax.ppermute(z, ("y", "z"), [(0, LAST)])

    mine, send = call(first_kernel, [half, half], [VM] * 8, BLOCK_SCRATCH, limit=16)(
        *zg, tab, wc, rows, w_qkv
    )
    w_fin_rows = w_fin.T

    def gathered_drifts(mine, send, z, *extra):
        peer = swap_cores(send)
        part, embed = call(
            own_kernel, [shape((S // 2, D), F32), shape((ROWS, D), F32)], [VM] * 5, limit=16
        )(send, mine, w_out, z, w_in)
        parts = call(sum_kernel, [row] * NX, [VM] * 3, limit=16)(part, peer, w_peer)
        got = [parts[0]] + [to_right(parts[k], k) for k in (2, 1, 3)]
        outs, *extra = call(
            drift_kernel,
            [shape((NY * NZ, 16, 128), BF), *extra],
            [SM, SM] + [VM] * 9,
        )(step_sizes, slide, high, state, embed, *got, rows, w_fin_rows)
        got = lax.all_to_all(outs, ("y", "z"), 0, 0, tiled=True)
        return got, *extra

    (got,) = gathered_drifts(mine, send, z)
    z, copies = call(
        state_kernel, [shape((16, 128), BF), shape((8, 16, 128), BF)], [VM] * 2
    )(z, got)
    zg = lax.all_to_all(copies, ("x", "c"), 0, 0, tiled=True)
    mine, send = call(second_kernel, [half, half], [VM] * 5, BLOCK_SCRATCH, limit=16)(
        zg, tab, wc, rows, w_qkv
    )
    got, target = gathered_drifts(mine, send, z, shape((8, 128), jnp.int32))
    return call(final_kernel, shape((1, ROWS, C), F32), [VM] * 2)(target, got)


def solution(mesh):
    grid = Mesh(mesh.devices.reshape(NY, NZ, NX, NC), ("y", "z", "x", "c"))
    step, head = ("y", "z"), ("x", "c")
    in_specs = (
        P(step, head, None),
        P(step),
        P(step),
        P(),
        P(),
        P(),
        P(),
        P(None, head),
        P(),
        P(head, None),
        P(),
    )
    out_specs = P(step, head, None)
    return jax.shard_map(local, mesh=grid, in_specs=in_specs, out_specs=out_specs, check_vma=False)
```

```python
import math

import jax
import jax.numpy as jnp
import numpy as np
from jax import lax
from jax.experimental import pallas as pl
from jax.experimental.pallas import tpu as pltpu
from jax.sharding import Mesh
from jax.sharding import PartitionSpec as P

NY, NZ, NX, NC = 4, 8, 4, 2
D = 3072
HD = 128
HL = 3
C = 64
S = 256
ROWS = 32
GRID_W = 16
ROT_DIM = 56
EPS = 1e-06
BF = jnp.bfloat16
F32 = jnp.float32
MIB = 1024 * 1024

VM = pl.BlockSpec(memory_space=pltpu.VMEM)
HB = pl.BlockSpec(memory_space=pltpu.HBM)
SM = pl.BlockSpec(memory_space=pltpu.SMEM)


def pack(x):
    return jnp.concatenate([x[:16], x[16:]], axis=1)


def unpack(x):
    return jnp.concatenate([x[:, :C], x[:, C:]], axis=0)


FREQ = [float(np.float32(10000.0 ** (-j * 2.0 / ROT_DIM))) for j in range(ROT_DIM // 2)]
QKV = 3 * HD


def swap_lanes(x):
    lane = lax.broadcasted_iota(jnp.int32, x.shape, len(x.shape) - 1)
    axis = len(x.shape) - 1
    return jnp.where(lane % 2 == 0, pltpu.roll(x, HD - 1, axis), pltpu.roll(x, 1, axis))


def halves(x):
    high = x.astype(BF)
    return high, (x - high.astype(F32)).astype(BF)


def stack_kernel(z, other, own):
    own[0] = z[...]
    own[1] = pack(other[0].astype(BF))


def prepare_kernel(
    step, after, offsets, gain, w_in, mod_table, w_qkv,
    tab, wc, rows, w_in_out, w_qkv_out,
    offv, gainv, modv, sems,
):
    at = jnp.clip(step[0], 0, mod_table.shape[1] - 1)
    block = pl.ds(pl.multiple_of(at // 8 * 8, 8), 8)
    pairs = [
        (offsets, offv),
        (gain, gainv),
        (w_in, w_in_out),
        (mod_table.at[:, block, :], modv),
        (w_qkv, w_qkv_out),
    ]
    copies = [pltpu.make_async_copy(a, b, sems.at[i]) for i, (a, b) in enumerate(pairs)]
    for copy in copies:
        copy.start()
    lane = lax.broadcasted_iota(jnp.int32, (1, HD), 1)
    pair = lane // 2
    by_row = jnp.zeros((1, HD), F32)
    by_col = jnp.zeros((1, HD), F32)
    count = ROT_DIM // 2
    for j in range(count):
        by_row = jnp.where(pair == HD // 2 - 2 * count + j, FREQ[j], by_row)
        by_col = jnp.where(pair == HD // 2 - count + j, FREQ[j], by_col)
    copies[0].wait()
    index = lax.broadcasted_iota(jnp.int32, (1, S), 1)
    row = (index // GRID_W + offv[0:1, :]).astype(F32)
    col = (index % GRID_W + offv[1:2, :]).astype(F32)
    both = jnp.concatenate([row, col, jnp.zeros((6, S), F32)], axis=0).T
    angle = both[:, 0:1] * by_row + both[:, 1:2] * by_col
    cosine = jnp.cos(angle)
    sine = jnp.sin(angle) * jnp.where(lane % 2 == 0, -1.0, 1.0)
    copies[1].wait()
    for k in range(2):
        g = gainv[k : k + 1, :]
        turned = swap_lanes(jnp.broadcast_to(g, (8, HD)))[0:1]
        tab[2 * k] = (cosine * g).reshape(8, ROWS, HD)
        tab[2 * k + 1] = (sine * turned).reshape(8, ROWS, HD)
    copies[2].wait()
    w = w_in_out[...].astype(F32)
    w = w - jnp.sum(w, axis=-1, keepdims=True) * (1.0 / D)
    high, low = halves(w)
    wc[:C, :] = high
    wc[C:, :] = low
    copies[3].wait()
    chosen = lax.broadcasted_iota(jnp.int32, (8, D), 0) == at % 8

    def pick(k):
        return jnp.sum(jnp.where(chosen, modv[k], 0.0), axis=0, keepdims=True)

    rows[0:1, :] = 1.0 + pick(1)
    rows[1:2, :] = pick(0)
    rows[2:3, :] = pick(2)
    rows[3:, :] = jnp.zeros((5, D), F32)
    for copy in copies[4:]:
        copy.wait()


PREPARE_SCRATCH = [
    pltpu.VMEM((2, S), jnp.int32),
    pltpu.VMEM((2, HD), F32),
    pltpu.VMEM((3, 8, D), F32),
    pltpu.SemaphoreType.DMA((5,)),
]


def attend(qs, low, high):
    scores = [
        lax.dot_general(
            qs[head, 0, low:high],
            qs[head, 1],
            (((1,), (1,)), ((), ())),
            preferred_element_type=F32,
        )
        for head in range(HL)
    ]
    tops = [jnp.max(score, axis=-1, keepdims=True) for score in scores]
    factor = math.log2(math.e) / math.sqrt(HD)
    probs = [jnp.exp2((score - top) * factor) for score, top in zip(scores, tops)]
    totals = [jnp.sum(p, axis=-1, keepdims=True) for p in probs]
    outs = [
        jnp.dot(p.astype(BF), qs[head, 2], preferred_element_type=F32)
        for head, p in enumerate(probs)
    ]
    outs = [(out * (1.0 / total)).astype(BF) for out, total in zip(outs, totals)]
    return jnp.concatenate(outs, axis=1)


def block_body(chunk_of, tab, wc, rows, w_qkv, send, qs, zs, es, fs, qkv):
    my_x, my_c = lax.axis_index("x"), lax.axis_index("c")
    order = [((my_x + r % 4) % 4) * 2 + (my_c + r // 4) % 2 for r in range(8)]
    for r in range(8):
        piece = chunk_of(r, order[r])
        zs[32 * r : 32 * r + 16, :] = piece[:, :C]
        zs[32 * r + 16 : 32 * r + 32, :] = piece[:, C:]
    z = zs[...]
    twice = jnp.concatenate([z, z], axis=1)
    total = jnp.zeros((S, 128), F32)
    for j in range(6):
        cut = slice(j * 512, j * 512 + 512)
        e = jnp.dot(twice, wc[:, cut], preferred_element_type=F32)
        es[:, cut] = e
        e = e * e
        total += (e[:, :128] + e[:, 128:256]) + (e[:, 256:384] + e[:, 384:])
    scale = lax.rsqrt(jnp.sum(total, axis=-1, keepdims=True) * (1.0 / D) + EPS)
    for j in range(6):
        cut = slice(j * 512, j * 512 + 512)
        fs[:, cut] = (es[:, cut] * scale * rows[0:1, cut] + rows[1:2, cut]).astype(BF)
    qkv[...] = jnp.dot(fs[...], w_qkv[...], preferred_element_type=F32)
    mean = jnp.full((2 * HD, HD), 1.0 / HD, BF)

    def table(k):
        return jnp.concatenate([tab[k, order[r]] for r in range(8)], axis=0)

    def turned(x, k):
        high, low = halves(x * x)
        square = jnp.dot(jnp.concatenate([high, low], axis=1), mean, preferred_element_type=F32)
        x = x * table(2 * k) + swap_lanes(x) * table(2 * k + 1)
        return (x * lax.rsqrt(square + EPS)).astype(BF)

    for head in range(HL):
        base = head * QKV
        for k in range(2):
            qs[head, k] = turned(qkv[:, base + k * HD : base + k * HD + HD], k)
        qs[head, 2] = qkv[:, base + 2 * HD : base + QKV].astype(BF)
    send[...] = attend(qs, S // 2, S)


def first_kernel(z0, z1, z2, z3, *rest):
    z = (z0, z1, z2, z3)
    block_body(lambda r, i: z[r % 4][r // 4], *rest)


def second_kernel(zg, *rest):
    block_body(lambda r, i: zg[i], *rest)


BLOCK_SCRATCH = [
    pltpu.VMEM((S, C), BF),
    pltpu.VMEM((S, D), F32),
    pltpu.VMEM((S, D), BF),
    pltpu.VMEM((S, HL * QKV), F32),
]


def own_kernel(after, qs, w_mine, z, w_in, out, embed):
    mine = attend(qs, 0, S // 2)
    embed[...] = jnp.dot(unpack(z[...]), w_in[...], preferred_element_type=F32)
    for j in range(6):
        cut = slice(j * 512, j * 512 + 512)
        out[:, cut] = jnp.dot(mine, w_mine[:, cut], preferred_element_type=F32)


def sum_kernel(part, peer, w_peer, *outs):
    for j in range(6):
        cut = slice(j * 512, j * 512 + 512)
        total = part[:, cut] + jnp.dot(peer[...], w_peer[:, cut], preferred_element_type=F32)
        total = total.astype(BF)
        for k in range(NX):
            outs[k][:, cut] = total[ROWS * k : ROWS * (k + 1)]


def position():
    return lax.axis_index("y") * NZ + lax.axis_index("z")


LAST = NY * NZ - 1


def drift_kernel(
    size, slide, high, zstart, embed, p0, p1, p2, p3, gate, w_fin, out, target=None
):
    attn = p0[...].astype(F32) + p1[...].astype(F32) + p2[...].astype(F32) + p3[...].astype(F32)
    h = embed[...] + gate[2:3, :] * attn
    mean = jnp.sum(h, axis=-1, keepdims=True) * (1.0 / D)
    h = h - mean
    var = jnp.sum(h * h, axis=-1, keepdims=True) * (1.0 / D)
    normed = (h * lax.rsqrt(var + EPS)).astype(BF)
    drift = size[0] * lax.dot_general(
        normed, w_fin[...], (((1,), (1,)), ((), ())), preferred_element_type=F32
    )
    here = position()
    low = zstart[...] - zstart[...].astype(BF).astype(F32)
    value = pack(drift + jnp.where(here == 0, low, 0.0)).astype(BF)
    value = jnp.where(here == LAST, high[...].astype(F32), value.astype(F32)).astype(BF)
    for k in range(out.shape[0]):
        out[k] = value
    if target is not None:
        target[...] = jnp.full((8, 128), jnp.minimum(here + slide[0], LAST), jnp.int32)


def summed(got, target):
    total = got[0].astype(F32) + got[LAST].astype(F32)
    for s in range(1, LAST):
        total = total + jnp.where(s < target, got[s].astype(F32), 0.0)
    return total


def state_kernel(z, got, z_out, copies):
    here = position()
    value = jnp.where(here == 0, z[...].astype(F32), summed(got, here)).astype(BF)
    z_out[...] = value
    for k in range(8):
        copies[k] = value


def final_kernel(target, got, out):
    out[0] = unpack(summed(got, jnp.concatenate([target[...], target[...]], axis=0)))


def call(body, out_shape, in_specs, scratch=(), limit=8):
    several = isinstance(out_shape, (list, tuple))
    return pl.pallas_call(
        body,
        out_shape=out_shape,
        in_specs=in_specs,
        out_specs=[VM] * len(out_shape) if several else VM,
        scratch_shapes=list(scratch),
        compiler_params=pltpu.CompilerParams(vmem_limit_bytes=limit * MIB),
    )


def shape(dims, dtype):
    return jax.ShapeDtypeStruct(dims, dtype)


def kept(dims, dtype):
    return pltpu.VMEM(dims, dtype)


def far(x):
    return pltpu.with_memory_space_constraint(x, pltpu.HBM)


def to_right(x, k):
    return lax.ppermute(x, "x", [(i, (i + k) % NX) for i in range(NX)])


def swap_cores(x):
    return lax.ppermute(x, "c", [(0, 1), (1, 0)])


def local(
    guesses, step_ids, step_sizes, slide, offsets, mod_table, w_in, w_qkv, qk_gain, w_out, w_fin
):
    state = guesses[0]
    z = pack(state.astype(BF))
    own = call(stack_kernel, shape((2, 16, 128), BF), [VM] * 2)(z, swap_cores(guesses))
    w_peer = swap_cores(lax.optimization_barrier((w_out, own))[0])
    zg = [own] + [to_right(own, NX - k) for k in range(1, NX)]
    operands = (offsets.T, qk_gain, w_in, mod_table.transpose(1, 0, 2), w_qkv)
    tab, wc, rows, w_in, w_qkv = call(
        prepare_kernel,
        [
            kept((4, 8, ROWS, HD), F32),
            kept((2 * C, D), BF),
            kept((8, D), F32),
            kept((C, D), BF),
            kept(w_qkv.shape, BF),
        ],
        [SM, VM] + [HB] * 5,
        PREPARE_SCRATCH,
        limit=12,
    )(step_ids, own, *[far(x) for x in operands])
    half = shape((S // 2, HL * HD), BF)
    row = shape((ROWS, D), BF)

    high = lax.ppermute(z, ("y", "z"), [(0, LAST)])

    send, qs = call(first_kernel, [half, shape((HL, 3, S, HD), BF)], [VM] * 8, BLOCK_SCRATCH, limit=16)(
        *zg, tab, wc, rows, w_qkv
    )
    w_fin_rows = w_fin.T

    def gathered_drifts(send, qs, z, *extra):
        peer = swap_cores(send)
        part, embed = call(
            own_kernel, [shape((S // 2, D), F32), shape((ROWS, D), F32)], [VM] * 5, limit=16
        )(send, qs, w_out, z, w_in)
        parts = call(sum_kernel, [row] * NX, [VM] * 3, limit=16)(part, peer, w_peer)
        got = [parts[0]] + [to_right(parts[k], k) for k in (2, 1, 3)]
        outs, *extra = call(
            drift_kernel,
            [shape((NY * NZ, 16, 128), BF), *extra],
            [SM, SM] + [VM] * 9,
        )(step_sizes, slide, high, state, embed, *got, rows, w_fin_rows)
        got = lax.all_to_all(outs, ("y", "z"), 0, 0, tiled=True)
        return got, *extra

    (got,) = gathered_drifts(send, qs, z)
    z, copies = call(
        state_kernel, [shape((16, 128), BF), shape((8, 16, 128), BF)], [VM] * 2
    )(z, got)
    zg = lax.all_to_all(copies, ("x", "c"), 0, 0, tiled=True)
    send, qs = call(second_kernel, [half, shape((HL, 3, S, HD), BF)], [VM] * 5, BLOCK_SCRATCH, limit=16)(
        zg, tab, wc, rows, w_qkv
    )
    got, target = gathered_drifts(send, qs, z, shape((8, 128), jnp.int32))
    return call(final_kernel, shape((1, ROWS, C), F32), [VM] * 2)(target, got)


def solution(mesh):
    grid = Mesh(mesh.devices.reshape(NY, NZ, NX, NC), ("y", "z", "x", "c"))
    step, head = ("y", "z"), ("x", "c")
    in_specs = (
        P(step, head, None),
        P(step),
        P(step),
        P(),
        P(),
        P(),
        P(),
        P(None, head),
        P(),
        P(head, None),
        P(),
    )
    out_specs = P(step, head, None)
    return jax.shard_map(local, mesh=grid, in_specs=in_specs, out_specs=out_specs, check_vma=False)
```

```python
import math

import jax
import jax.numpy as jnp
import numpy as np
from jax import lax
from jax.experimental import pallas as pl
from jax.experimental.pallas import tpu as pltpu
from jax.sharding import Mesh
from jax.sharding import PartitionSpec as P

NY, NZ, NX, NC = 4, 8, 4, 2
D = 3072
HD = 128
HL = 3
C = 64
S = 256
ROWS = 32
GRID_W = 16
ROT_DIM = 56
EPS = 1e-06
BF = jnp.bfloat16
F32 = jnp.float32
MIB = 1024 * 1024

VM = pl.BlockSpec(memory_space=pltpu.VMEM)
HB = pl.BlockSpec(memory_space=pltpu.HBM)
SM = pl.BlockSpec(memory_space=pltpu.SMEM)


def pack(x):
    return jnp.concatenate([x[:16], x[16:]], axis=1)


def unpack(x):
    return jnp.concatenate([x[:, :C], x[:, C:]], axis=0)


FREQ = [float(np.float32(10000.0 ** (-j * 2.0 / ROT_DIM))) for j in range(ROT_DIM // 2)]
QKV = 3 * HD


def swap_lanes(x):
    lane = lax.broadcasted_iota(jnp.int32, x.shape, len(x.shape) - 1)
    axis = len(x.shape) - 1
    return jnp.where(lane % 2 == 0, pltpu.roll(x, HD - 1, axis), pltpu.roll(x, 1, axis))


def halves(x):
    high = x.astype(BF)
    return high, (x - high.astype(F32)).astype(BF)


def stack_kernel(z, other, own):
    own[0] = z[...]
    own[1] = pack(other[0].astype(BF))


def prepare_kernel(
    step, after, offsets, gain, w_in, mod_table, w_qkv,
    tab, wc, rows, w_in_out, w_qkv_out,
    offv, gainv, modv, sems,
):
    at = jnp.clip(step[0], 0, mod_table.shape[1] - 1)
    block = pl.ds(pl.multiple_of(at // 8 * 8, 8), 8)
    pairs = [
        (offsets, offv),
        (gain, gainv),
        (w_in, w_in_out),
        (mod_table.at[:, block, :], modv),
        (w_qkv, w_qkv_out),
    ]
    copies = [pltpu.make_async_copy(a, b, sems.at[i]) for i, (a, b) in enumerate(pairs)]
    for copy in copies:
        copy.start()
    lane = lax.broadcasted_iota(jnp.int32, (1, HD), 1)
    pair = lane // 2
    by_row = jnp.zeros((1, HD), F32)
    by_col = jnp.zeros((1, HD), F32)
    count = ROT_DIM // 2
    for j in range(count):
        by_row = jnp.where(pair == HD // 2 - 2 * count + j, FREQ[j], by_row)
        by_col = jnp.where(pair == HD // 2 - count + j, FREQ[j], by_col)
    copies[0].wait()
    index = lax.broadcasted_iota(jnp.int32, (1, S), 1)
    row = (index // GRID_W + offv[0:1, :]).astype(F32)
    col = (index % GRID_W + offv[1:2, :]).astype(F32)
    both = jnp.concatenate([row, col, jnp.zeros((6, S), F32)], axis=0).T
    angle = both[:, 0:1] * by_row + both[:, 1:2] * by_col
    cosine = jnp.cos(angle)
    sine = jnp.sin(angle) * jnp.where(lane % 2 == 0, -1.0, 1.0)
    copies[1].wait()
    for k in range(2):
        g = gainv[k : k + 1, :]
        turned = swap_lanes(jnp.broadcast_to(g, (8, HD)))[0:1]
        tab[2 * k] = (cosine * g).reshape(8, ROWS, HD)
        tab[2 * k + 1] = (sine * turned).reshape(8, ROWS, HD)
    copies[2].wait()
    w = w_in_out[...].astype(F32)
    w = w - jnp.sum(w, axis=-1, keepdims=True) * (1.0 / D)
    high, low = halves(w)
    wc[:C, :] = high
    wc[C:, :] = low
    copies[3].wait()
    chosen = lax.broadcasted_iota(jnp.int32, (8, D), 0) == at % 8

    def pick(k):
        return jnp.sum(jnp.where(chosen, modv[k], 0.0), axis=0, keepdims=True)

    rows[0:1, :] = 1.0 + pick(1)
    rows[1:2, :] = pick(0)
    rows[2:3, :] = pick(2)
    rows[3:, :] = jnp.zeros((5, D), F32)
    for copy in copies[4:]:
        copy.wait()


PREPARE_SCRATCH = [
    pltpu.VMEM((2, S), jnp.int32),
    pltpu.VMEM((2, HD), F32),
    pltpu.VMEM((3, 8, D), F32),
    pltpu.SemaphoreType.DMA((5,)),
]


def block_body(chunk_of, tab, wc, rows, w_qkv, mine, send, zs, es, fs, qkv, qs):
    my_x, my_c = lax.axis_index("x"), lax.axis_index("c")
    order = [((my_x + r % 4) % 4) * 2 + (my_c + r // 4) % 2 for r in range(8)]
    for r in range(8):
        piece = chunk_of(r, order[r])
        zs[32 * r : 32 * r + 16, :] = piece[:, :C]
        zs[32 * r + 16 : 32 * r + 32, :] = piece[:, C:]
    z = zs[...]
    twice = jnp.concatenate([z, z], axis=1)
    total = jnp.zeros((S, 128), F32)
    for j in range(6):
        cut = slice(j * 512, j * 512 + 512)
        e = jnp.dot(twice, wc[:, cut], preferred_element_type=F32)
        es[:, cut] = e
        e = e * e
        total += (e[:, :128] + e[:, 128:256]) + (e[:, 256:384] + e[:, 384:])
    scale = lax.rsqrt(jnp.sum(total, axis=-1, keepdims=True) * (1.0 / D) + EPS)
    for j in range(6):
        cut = slice(j * 512, j * 512 + 512)
        fs[:, cut] = (es[:, cut] * scale * rows[0:1, cut] + rows[1:2, cut]).astype(BF)
    qkv[...] = jnp.dot(fs[...], w_qkv[...], preferred_element_type=F32)
    mean = jnp.full((2 * HD, HD), 1.0 / HD, BF)

    def table(k):
        return jnp.concatenate([tab[k, order[r]] for r in range(8)], axis=0)

    def turned(x, k):
        high, low = halves(x * x)
        square = jnp.dot(jnp.concatenate([high, low], axis=1), mean, preferred_element_type=F32)
        x = x * table(2 * k) + swap_lanes(x) * table(2 * k + 1)
        return (x * lax.rsqrt(square + EPS)).astype(BF)

    for head in range(HL):
        base = head * QKV
        for k in range(2):
            qs[head, k] = turned(qkv[:, base + k * HD : base + k * HD + HD], k)
        qs[head, 2] = qkv[:, base + 2 * HD : base + QKV].astype(BF)
    scores = [
        lax.dot_general(
            qs[head, 0], qs[head, 1], (((1,), (1,)), ((), ())), preferred_element_type=F32
        )
        for head in range(HL)
    ]
    tops = [jnp.max(score, axis=-1, keepdims=True) for score in scores]
    factor = math.log2(math.e) / math.sqrt(HD)
    probs = [jnp.exp2((score - top) * factor) for score, top in zip(scores, tops)]
    totals = [jnp.sum(p, axis=-1, keepdims=True) for p in probs]
    outs = [
        jnp.dot(p.astype(BF), qs[head, 2], preferred_element_type=F32)
        for head, p in enumerate(probs)
    ]
    for head in range(HL):
        out = (outs[head] * (1.0 / totals[head])).astype(BF)
        mine[:, head * HD : head * HD + HD] = out[: S // 2]
        send[:, head * HD : head * HD + HD] = out[S // 2 :]


def first_kernel(z0, z1, z2, z3, *rest):
    z = (z0, z1, z2, z3)
    block_body(lambda r, i: z[r % 4][r // 4], *rest)


def second_kernel(zg, *rest):
    block_body(lambda r, i: zg[i], *rest)


BLOCK_SCRATCH = [
    pltpu.VMEM((S, C), BF),
    pltpu.VMEM((S, D), F32),
    pltpu.VMEM((S, D), BF),
    pltpu.VMEM((S, HL * QKV), F32),
    pltpu.VMEM((HL, 3, S, HD), BF),
]


def own_kernel(after, mine, w_mine, z, w_in, out, embed):
    embed[...] = jnp.dot(unpack(z[...]), w_in[...], preferred_element_type=F32)
    for j in range(6):
        cut = slice(j * 512, j * 512 + 512)
        out[:, cut] = jnp.dot(mine[...], w_mine[:, cut], preferred_element_type=F32)


def sum_kernel(part, peer, w_peer, *outs):
    even = lax.axis_index("c") == 0
    for j in range(6):
        cut = slice(j * 512, j * 512 + 512)
        total = part[:, cut] + jnp.dot(peer[...], w_peer[:, cut], preferred_element_type=F32)
        total = total.astype(BF)
        for k in (0, 2):
            outs[k][:, cut] = total[ROWS * k : ROWS * (k + 1)]
        right, left = total[ROWS : 2 * ROWS], total[3 * ROWS :]
        outs[1][:, cut] = jnp.where(even, right, left)
        outs[3][:, cut] = jnp.where(even, left, right)


def position():
    return lax.axis_index("y") * NZ + lax.axis_index("z")


LAST = NY * NZ - 1


def drift_kernel(
    size, slide, high, zstart, embed, p0, p1, p2, p3, gate, w_fin, out, target=None
):
    attn = p0[...].astype(F32) + p1[...].astype(F32) + p2[...].astype(F32) + p3[...].astype(F32)
    h = embed[...] + gate[2:3, :] * attn
    mean = jnp.sum(h, axis=-1, keepdims=True) * (1.0 / D)
    h = h - mean
    var = jnp.sum(h * h, axis=-1, keepdims=True) * (1.0 / D)
    normed = (h * lax.rsqrt(var + EPS)).astype(BF)
    drift = size[0] * lax.dot_general(
        normed, w_fin[...], (((1,), (1,)), ((), ())), preferred_element_type=F32
    )
    here = position()
    low = zstart[...] - zstart[...].astype(BF).astype(F32)
    value = pack(drift + jnp.where(here == 0, low, 0.0)).astype(BF)
    value = jnp.where(here == LAST, high[...].astype(F32), value.astype(F32)).astype(BF)
    for k in range(out.shape[0]):
        out[k] = value
    if target is not None:
        target[...] = jnp.full((8, 128), jnp.minimum(here + slide[0], LAST), jnp.int32)


def summed(got, target):
    total = got[0].astype(F32) + got[LAST].astype(F32)
    for s in range(1, LAST):
        total = total + jnp.where(s < target, got[s].astype(F32), 0.0)
    return total


def state_kernel(z, got, z_out, copies):
    here = position()
    value = jnp.where(here == 0, z[...].astype(F32), summed(got, here)).astype(BF)
    z_out[...] = value
    for k in range(8):
        copies[k] = value


def final_kernel(target, got, out):
    out[0] = unpack(summed(got, jnp.concatenate([target[...], target[...]], axis=0)))


def call(body, out_shape, in_specs, scratch=(), limit=8):
    several = isinstance(out_shape, (list, tuple))
    return pl.pallas_call(
        body,
        out_shape=out_shape,
        in_specs=in_specs,
        out_specs=[VM] * len(out_shape) if several else VM,
        scratch_shapes=list(scratch),
        compiler_params=pltpu.CompilerParams(vmem_limit_bytes=limit * MIB),
    )


def shape(dims, dtype):
    return jax.ShapeDtypeStruct(dims, dtype)


def kept(dims, dtype):
    return pltpu.VMEM(dims, dtype)


def far(x):
    return pltpu.with_memory_space_constraint(x, pltpu.HBM)


def to_right(x, k):
    return lax.ppermute(x, "x", [(i, (i + k) % NX) for i in range(NX)])


def apart(x, k):
    pairs = [(i * NC + c, (i + (k if c == 0 else -k)) % NX * NC + c) for i in range(NX) for c in range(NC)]
    return lax.ppermute(x, ("x", "c"), pairs)


def swap_cores(x):
    return lax.ppermute(x, "c", [(0, 1), (1, 0)])


def local(
    guesses, step_ids, step_sizes, slide, offsets, mod_table, w_in, w_qkv, qk_gain, w_out, w_fin
):
    state = guesses[0]
    z = pack(state.astype(BF))
    own = call(stack_kernel, shape((2, 16, 128), BF), [VM] * 2)(z, swap_cores(guesses))
    w_peer = swap_cores(lax.optimization_barrier((w_out, own))[0])
    zg = [own] + [to_right(own, NX - k) for k in range(1, NX)]
    operands = (offsets.T, qk_gain, w_in, mod_table.transpose(1, 0, 2), w_qkv)
    tab, wc, rows, w_in, w_qkv = call(
        prepare_kernel,
        [
            kept((4, 8, ROWS, HD), F32),
            kept((2 * C, D), BF),
            kept((8, D), F32),
            kept((C, D), BF),
            kept(w_qkv.shape, BF),
        ],
        [SM, VM] + [HB] * 5,
        PREPARE_SCRATCH,
        limit=12,
    )(step_ids, own, *[far(x) for x in operands])
    half = shape((S // 2, HL * HD), BF)
    row = shape((ROWS, D), BF)

    high = lax.ppermute(z, ("y", "z"), [(0, LAST)])

    mine, send = call(first_kernel, [half, half], [VM] * 8, BLOCK_SCRATCH, limit=16)(
        *zg, tab, wc, rows, w_qkv
    )
    w_fin_rows = w_fin.T

    def gathered_drifts(mine, send, z, *extra):
        peer = swap_cores(send)
        part, embed = call(
            own_kernel, [shape((S // 2, D), F32), shape((ROWS, D), F32)], [VM] * 5, limit=16
        )(send, mine, w_out, z, w_in)
        parts = call(sum_kernel, [row] * NX, [VM] * 3, limit=16)(part, peer, w_peer)
        got = [parts[0], to_right(parts[2], 2), apart(parts[1], 1), apart(parts[3], -1)]
        outs, *extra = call(
            drift_kernel,
            [shape((NY * NZ, 16, 128), BF), *extra],
            [SM, SM] + [VM] * 9,
        )(step_sizes, slide, high, state, embed, *got, rows, w_fin_rows)
        got = lax.all_to_all(outs, ("y", "z"), 0, 0, tiled=True)
        return got, *extra

    (got,) = gathered_drifts(mine, send, z)
    z, copies = call(
        state_kernel, [shape((16, 128), BF), shape((8, 16, 128), BF)], [VM] * 2
    )(z, got)
    zg = lax.all_to_all(copies, ("x", "c"), 0, 0, tiled=True)
    mine, send = call(second_kernel, [half, half], [VM] * 5, BLOCK_SCRATCH, limit=16)(
        zg, tab, wc, rows, w_qkv
    )
    got, target = gathered_drifts(mine, send, z, shape((8, 128), jnp.int32))
    return call(final_kernel, shape((1, ROWS, C), F32), [VM] * 2)(target, got)


def solution(mesh):
    grid = Mesh(mesh.devices.reshape(NY, NZ, NX, NC), ("y", "z", "x", "c"))
    step, head = ("y", "z"), ("x", "c")
    in_specs = (
        P(step, head, None),
        P(step),
        P(step),
        P(),
        P(),
        P(),
        P(),
        P(None, head),
        P(),
        P(head, None),
        P(),
    )
    out_specs = P(step, head, None)
    return jax.shard_map(local, mesh=grid, in_specs=in_specs, out_specs=out_specs, check_vma=False)
```
